128 devices in a mesh: space: 32 (over x, y_lo, z), frame: 4 (over y_hi, core).
Axes of the slice: x: 4, y: 4 (y_hi: 2, y_lo: 2; y = y_hi * 2 + y_lo), z: 4, core: 2. Of those that a mesh axis runs over, the one named last changes fastest.
Arguments:
- queries: bfloat16 [9216, 4096], P(('space', 'frame')), may hold values from -50 to 50
- keys_now: bfloat16 [9216, 4096], P(('space', 'frame')), may hold values from -6 to 6
- values_now: bfloat16 [9216, 4096], P(('space', 'frame')), may hold values from -4 to 4
- keys_base: bfloat16 [9216, 4096], P(('space', 'frame')), may hold values from -4 to 4
- values_base: bfloat16 [9216, 4096], P(('space', 'frame')), may hold values from -4 to 4
- scale_codes: int32 [9216, 64], P(('space', 'frame')), may hold values from -10 to -7
Outputs:
- attended: bfloat16 [9216, 4096], P(('space', 'frame'))
The draws below stay inside these ranges and needn't reach their ends.
All inputs are finite; a program needn't handle non-finite values.
Results may differ from the reference program's by a relative error of at most 0.013.
Values may be sent and summed in bfloat16 or wider, within the bound.
No kernel may reach another device: no remote copies, remote signals or barrier semaphores. Data moves between devices by JAX's collectives and lax.ppermute only.
A program may use at most 256 MiB of HBM per device.

```python
import jax
import jax.numpy as jnp
from jax import lax

H = 32
HD = 128
TOKENS = 9216
N_SPACE = 32


def shared_fields(key):
    key_stale = jax.random.fold_in(key, 11)
    key_drift = jax.random.fold_in(key, 13)
    key_query = jax.random.fold_in(key, 17)
    columns = H * HD
    old_keys = jnp.clip(jax.random.normal(key_stale, (TOKENS, columns), jnp.float32), -4.0, 4.0)
    drifts = 0.5 * jnp.clip(jax.random.normal(key_drift, (TOKENS, columns), jnp.float32), -4.0, 4.0)
    query_draw = 2.5 * jnp.clip(jax.random.normal(key_query, (TOKENS, columns), jnp.float32), -4.0, 4.0)
    old_keys = old_keys.astype(jnp.bfloat16).astype(jnp.float32)
    return (old_keys, old_keys + drifts, query_draw)


def draw_queries(key, part):
    return shared_fields(key)[2].astype(jnp.bfloat16)


def draw_keys_now(key, part):
    return shared_fields(key)[1].astype(jnp.bfloat16)


def draw_keys_base(key, part):
    return shared_fields(key)[0].astype(jnp.bfloat16)


def with_ends(values, stream_key, smallest, top_value):
    place = [jax.random.randint(jax.random.fold_in(stream_key, axis), (), 0, length) for axis, length in enumerate(values.shape)]
    main_axis = values.shape.index(max(values.shape))
    next_to = place[:main_axis] + [(place[main_axis] + 1) % values.shape[main_axis]] + place[main_axis + 1:]
    return values.at[tuple(place)].set(smallest).at[tuple(next_to)].set(top_value)


def shard_levels(key, dims, cuts, smallest, top_value):
    level, own = 1.0, jax.random.fold_in(key, 6)
    for axis_at, blocks in cuts:
        heights = jnp.exp(jax.random.uniform(jax.random.fold_in(own, axis_at), (blocks,), jnp.float32, smallest / len(cuts), top_value / len(cuts)))
        level = level * jnp.repeat(heights, dims[axis_at] // blocks).reshape([-1 if axis == axis_at else 1 for axis in range(len(dims))])
    return level


def normal_values(rng, dims, spread, reach, cuts=(), dtype=jnp.bfloat16):
    level = shard_levels(rng, dims, cuts, -0.22, 0.18) if cuts else 1.0
    entries = jax.random.normal(rng, dims, jnp.float32) * spread * level
    return jnp.minimum(jnp.maximum(entries, -reach), reach).astype(dtype)


def setup_inputs(seed: int = 0) -> dict:
    key_of = jax.random.split(jax.random.key(seed), 7)
    return {
        "queries": draw_queries(jax.random.fold_in(key_of[6], 71), 0),
        "keys_now": draw_keys_now(jax.random.fold_in(key_of[6], 71), 0),
        "values_now": normal_values(key_of[2], (TOKENS, H * HD), 1.0, 4.0, ((0, 128),)),
        "keys_base": draw_keys_base(jax.random.fold_in(key_of[6], 71), 0),
        "values_base": normal_values(key_of[4], (TOKENS, H * HD), 1.0, 4.0, ((0, 128),)),
        "scale_codes": with_ends(jax.random.randint(key_of[5], (TOKENS, 2 * H), -10, -6), jax.random.fold_in(key_of[5], 1), -10, (-6) - 1).astype(jnp.int32),
    }


SATURATE = 448.0


def powers_of_two(exponents):
    return jnp.left_shift(jnp.ones_like(exponents), exponents + 16).astype(jnp.float32) * (1.0 / 65536.0)


def encode(current, stale_rows, exponents, head_size):
    shrink = jnp.repeat(65536.0 / jnp.left_shift(jnp.ones_like(exponents), exponents + 16).astype(jnp.float32), head_size, axis=1)
    change = current.astype(jnp.float32) - stale_rows.astype(jnp.float32)
    return jnp.clip(change * shrink, -SATURATE, SATURATE).astype(jnp.bfloat16)


def decode(stale_rows, packed, exponents, head_size):
    growth = jnp.repeat(powers_of_two(exponents), head_size, axis=1)
    return (stale_rows.astype(jnp.float32) + growth * packed.astype(jnp.float32)).astype(jnp.bfloat16)


def attend(queries, keys, values):
    token_count = queries.shape[0]

    def by_head(tensor):
        return tensor.reshape(token_count, H, HD).transpose(1, 0, 2)

    block_rows = token_count // N_SPACE

    def one_head(operands):
        query_head, key_head, value_head = operands

        def one_block(query_block):
            scores = jnp.dot(query_block, key_head.T, preferred_element_type=jnp.float32) * (HD ** -0.5)
            largest = jnp.max(scores, axis=1, keepdims=True)
            expo = jnp.exp(scores - largest)
            totals = jnp.sum(expo, axis=1, keepdims=True)
            weights = expo.astype(jnp.bfloat16)
            return (jnp.dot(weights, value_head, preferred_element_type=jnp.float32) / totals).astype(jnp.bfloat16)

        blocks = query_head.reshape(token_count // block_rows, block_rows, HD)
        return lax.map(one_block, blocks).reshape(token_count, HD)

    outputs = lax.map(one_head, (by_head(queries), by_head(keys), by_head(values)))
    return outputs.transpose(1, 0, 2).reshape(token_count, H * HD)


def reference(queries, keys_now, values_now, keys_base, values_base, scale_codes):
    key_codes = scale_codes[:, 0::2]
    value_codes = scale_codes[:, 1::2]
    keys = decode(keys_base, encode(keys_now, keys_base, key_codes, HD), key_codes, HD)
    values = decode(values_base, encode(values_now, values_base, value_codes, HD), value_codes, HD)
    return attend(queries, keys, values)
```

```python
import functools

import jax
import jax.numpy as jnp
from jax import lax
from jax.experimental import pallas as pl
from jax.experimental.pallas import tpu as pltpu
from jax.sharding import Mesh
from jax.sharding import PartitionSpec as P

HEADS = 32
HD = 128
ROWS = 72
PEERS = 64
SATURATE = 448.0
LOGIT = 128 ** -0.5 * 1.4426950408889634
Q_ROWS = 40
QN = HEADS * ROWS
SUMS = 16
SLACK = 64.0
BQ = 768
BK = 768
f32 = jnp.float32
bf16 = jnp.bfloat16


def pick_columns(first, count, parity):
    row = lax.broadcasted_iota(jnp.int32, (2 * HEADS, count * HD), 0)
    col = lax.broadcasted_iota(jnp.int32, (2 * HEADS, count * HD), 1)
    return (row == 2 * (first + col // HD) + parity).astype(f32).astype(bf16)


def rebuild(now, base, growth, shrink):
    base = base.astype(f32)
    residual = jnp.clip((now.astype(f32) - base) * shrink, -SATURATE, SATURATE)
    return (base + growth * residual.astype(bf16).astype(f32)).astype(bf16).astype(f32)


def pack_kernel(heads, q_ref, kn_ref, vn_ref, kb_ref, vb_ref, code_ref, out_ref):
    first = pl.program_id(0) * heads
    codes = code_ref[...]
    one = jnp.ones_like(codes)
    up = (jnp.left_shift(one, codes + 16).astype(f32) * (1.0 / 65536.0)).astype(bf16)
    down = jnp.left_shift(one, -codes).astype(f32).astype(bf16)
    made = []
    for parity, now_ref, base_ref in ((0, kn_ref, kb_ref), (1, vn_ref, vb_ref)):
        pick = pick_columns(first, heads, parity)
        growth = jnp.dot(up, pick, preferred_element_type=f32)
        shrink = jnp.dot(down, pick, preferred_element_type=f32)
        made.append(rebuild(now_ref[...], base_ref[...], growth, shrink))
    keys, values = made
    queries = q_ref[...].astype(f32)
    for h in range(heads):
        cols = slice(h * HD, (h + 1) * HD)
        k, v, q = keys[:, cols], values[:, cols], queries[:, cols]
        out_ref[2 * h] = jnp.concatenate([k, v, q[0:40]], axis=0).astype(bf16)
        out_ref[2 * h + 1] = jnp.concatenate([k, v, q[40:72], q[32:40]], axis=0).astype(bf16)


def pack(queries, keys_now, values_now, keys_base, values_base, codes):
    heads = 4
    wide = pl.BlockSpec((ROWS, heads * HD), lambda i: (0, i))
    return pl.pallas_call(
        functools.partial(pack_kernel, heads),
        grid=(HEADS // heads,),
        in_specs=[wide] * 5 + [pl.BlockSpec((ROWS, 2 * HEADS), lambda i: (0, 0))],
        out_specs=pl.BlockSpec((2 * heads, 2 * ROWS + Q_ROWS, HD), lambda i: (i, 0, 0)),
        out_shape=jax.ShapeDtypeStruct((PEERS, 2 * ROWS + Q_ROWS, HD), bf16),
        compiler_params=pltpu.CompilerParams(vmem_limit_bytes=32 * 2**20),
        name="pack",
    )(queries, keys_now, values_now, keys_base, values_base, codes)


def lay_out(rec_ref, tokens, k_ref, vt_ref, at):
    group = 16
    count = group * tokens

    def step(g, carry):
        part = rec_ref[pl.ds(g * group, group)].astype(f32)
        keys = part[:, 0:tokens].reshape(count, HD)
        values = part[:, tokens : 2 * tokens].reshape(count, HD)
        start = pl.multiple_of(at + g * count, HD)
        k_ref[pl.ds(start, count), :] = keys.astype(bf16)
        vt_ref[0:HD, pl.ds(start, count)] = values.T.astype(bf16)
        return carry

    lax.fori_loop(0, PEERS // group, step, 0)


def lay_out_queries(rec_ref, from_row, mine, q_ref):
    group = 8

    def step(g, carry):
        part = rec_ref[pl.ds(2 * g * group, 2 * group)].astype(f32)
        part = part[:, from_row : from_row + Q_ROWS].reshape(group, 2 * Q_ROWS, HD)
        shared = jnp.where(mine == 0, part[:, 32:40], part[:, 72:80])
        rows = jnp.concatenate([part[:, 0:32], part[:, 40:72], shared], axis=1)
        rows = rows.reshape(group * ROWS, HD) * LOGIT
        high = rows.astype(bf16)
        low = (rows - high.astype(f32)).astype(bf16)
        start = pl.multiple_of(g * group * ROWS, 64)
        q_ref[pl.ds(start, group * ROWS), :] = jnp.concatenate([high, low], axis=1)
        return carry

    lax.fori_loop(0, HEADS // group, step, 0)


def attend_kernel(mine_ref, own_ref, other_ref, out_ref, q_ref, k_ref, vt_ref, o_ref):
    kv = k_ref.shape[0]
    mine = mine_ref[0]
    lay_out_queries(own_ref, 2 * ROWS, mine, q_ref)
    lay_out(own_ref, ROWS, k_ref, vt_ref, 0)
    lay_out(other_ref, ROWS, k_ref, vt_ref, kv // 2)
    vt_ref[HD : HD + SUMS, :] = jnp.ones((SUMS, kv), bf16)
    blocks = kv // BK

    def one_block(b, carry):
        rows = pl.ds(pl.multiple_of(b * BQ, BQ), BQ)
        q = q_ref[rows, :]

        def scores(j):
            if isinstance(j, int):
                k = k_ref[j * BK : (j + 1) * BK, :]
            else:
                k = k_ref[pl.ds(pl.multiple_of(j * BK, BK), BK), :]
            k = jnp.concatenate([k, k], axis=1)
            return lax.dot_general(k, q, (((1,), (1,)), ((), ())), preferred_element_type=f32)

        def weigh(j, s, shift):
            if isinstance(j, int):
                v = vt_ref[:, j * BK : (j + 1) * BK]
            else:
                v = vt_ref[:, pl.ds(pl.multiple_of(j * BK, BK), BK)]
            return jnp.dot(v, jnp.exp2(s - shift).astype(bf16), preferred_element_type=f32)

        def finish(total):
            o_ref[rows, :] = (total[:HD] / total[HD : HD + 1]).T

        s = scores(0)
        shift = jnp.max(s, axis=0, keepdims=True)
        largest = shift
        total = None
        for j in range(blocks):
            coming = scores(j + 1) if j + 1 < blocks else None
            if j:
                largest = jnp.maximum(largest, jnp.max(s, axis=0, keepdims=True))
            part = weigh(j, s, shift)
            total = part if total is None else total + part
            s = coming
        finish(total)

        @pl.when(jnp.max(largest - shift) > SLACK)
        def _():
            def step(j, held):
                top, total = held
                s = scores(j)
                newer = jnp.maximum(top, jnp.max(s, axis=0, keepdims=True))
                return newer, total * jnp.exp2(top - newer) + weigh(j, s, newer)

            start = (jnp.full((1, BQ), -jnp.inf, f32), jnp.zeros((HD + SUMS, BQ), f32))
            finish(lax.fori_loop(0, blocks, step, start)[1])

        return carry

    lax.fori_loop(0, QN // BQ, one_block, 0)

    def send(s, carry):
        rows = o_ref[pl.ds(pl.multiple_of(s * ROWS, 8), ROWS), :]
        out_ref[2 * s] = jnp.concatenate([rows[0:32], rows[64:72]], axis=0).astype(bf16)
        out_ref[2 * s + 1] = rows[32:72].astype(bf16)
        return carry

    lax.fori_loop(0, HEADS, send, 0)


def attend(mine, own, other):
    kv = 2 * PEERS * ROWS
    vmem = pl.BlockSpec(memory_space=pltpu.VMEM)
    return pl.pallas_call(
        attend_kernel,
        in_specs=[pl.BlockSpec(memory_space=pltpu.SMEM), vmem, vmem],
        out_specs=vmem,
        out_shape=jax.ShapeDtypeStruct((PEERS, Q_ROWS, HD), bf16),
        scratch_shapes=[
            pltpu.VMEM((QN, 2 * HD), bf16),
            pltpu.VMEM((kv, HD), bf16),
            pltpu.VMEM((HD + SUMS, kv), bf16),
            pltpu.VMEM((QN, HD), f32),
        ],
        compiler_params=pltpu.CompilerParams(vmem_limit_bytes=48 * 2**20),
        name="attend",
    )(mine, own, other)


def unpack_kernel(heads, mine_ref, rec_ref, out_ref):
    mine = mine_ref[0]
    for h in range(heads):
        low, high = rec_ref[2 * h].astype(f32), rec_ref[2 * h + 1].astype(f32)
        shared = jnp.where(mine == 0, low[32:40], high[32:40])
        rows = jnp.concatenate([low[0:32], shared, high[0:32]], axis=0)
        out_ref[:, h * HD : (h + 1) * HD] = rows.astype(bf16)


def unpack(mine, received):
    heads = 8
    return pl.pallas_call(
        functools.partial(unpack_kernel, heads),
        grid=(HEADS // heads,),
        in_specs=[
            pl.BlockSpec(memory_space=pltpu.SMEM),
            pl.BlockSpec((2 * heads, Q_ROWS, HD), lambda i: (i, 0, 0)),
        ],
        out_specs=pl.BlockSpec((ROWS, heads * HD), lambda i: (0, i)),
        out_shape=jax.ShapeDtypeStruct((ROWS, HEADS * HD), bf16),
        name="unpack",
    )(mine, received)


def exchange(messages):
    return lax.all_to_all(messages, ("space", "yhi"), split_axis=0, concat_axis=0, tiled=True)


def per_device(queries, keys_now, values_now, keys_base, values_base, scale_codes):
    mine = lax.axis_index("yhi").astype(jnp.int32).reshape(1)
    own = exchange(pack(queries, keys_now, values_now, keys_base, values_base, scale_codes))
    other = lax.ppermute(own, "core", [(0, 1), (1, 0)])
    return unpack(mine, exchange(attend(mine, own, other)))


def solution(mesh):
    finer = Mesh(mesh.devices.reshape(HEADS, 2, 2), ("space", "yhi", "core"))
    rows = P(("space", "yhi", "core"), None)
    return jax.shard_map(
        per_device, mesh=finer, in_specs=(rows,) * 6, out_specs=rows, check_vma=False
    )
```

```python
import functools

import jax
import jax.numpy as jnp
from jax import lax
from jax.experimental import pallas as pl
from jax.experimental.pallas import tpu as pltpu
from jax.sharding import Mesh
from jax.sharding import PartitionSpec as P

HEADS = 32
HD = 128
ROWS = 72
SATURATE = 448.0
LOGIT = 128 ** -0.5 * 1.4426950408889634
CHUNKS = 3
CROWS = ROWS // CHUNKS
BQ = HEADS * CROWS
QN = HEADS * ROWS
KV = HEADS * ROWS
SUMS = 16
SLACK = 64.0
BK = 768
f32 = jnp.float32
bf16 = jnp.bfloat16


def pick_columns(first, count, parity):
    row = lax.broadcasted_iota(jnp.int32, (2 * HEADS, count * HD), 0)
    col = lax.broadcasted_iota(jnp.int32, (2 * HEADS, count * HD), 1)
    return (row == 2 * (first + col // HD) + parity).astype(f32).astype(bf16)


def rebuild(now, base, growth, shrink):
    base = base.astype(f32)
    residual = jnp.clip((now.astype(f32) - base) * shrink, -SATURATE, SATURATE)
    return (base + growth * residual.astype(bf16).astype(f32)).astype(bf16).astype(f32)


def pack_kernel(heads, q_ref, kn_ref, vn_ref, kb_ref, vb_ref, code_ref, out_ref):
    first = pl.program_id(0) * heads
    codes = code_ref[...]
    one = jnp.ones_like(codes)
    up = (jnp.left_shift(one, codes + 16).astype(f32) * (1.0 / 65536.0)).astype(bf16)
    down = jnp.left_shift(one, -codes).astype(f32).astype(bf16)
    made = []
    for parity, now_ref, base_ref in ((0, kn_ref, kb_ref), (1, vn_ref, vb_ref)):
        pick = pick_columns(first, heads, parity)
        growth = jnp.dot(up, pick, preferred_element_type=f32)
        shrink = jnp.dot(down, pick, preferred_element_type=f32)
        made.append(rebuild(now_ref[...], base_ref[...], growth, shrink))
    keys, values = made
    queries = q_ref[...].astype(f32)
    for h in range(heads):
        cols = slice(h * HD, (h + 1) * HD)
        message = [keys[:, cols], values[:, cols], queries[:, cols]]
        out_ref[h] = jnp.concatenate(message, axis=0).astype(bf16)


def pack(queries, keys_now, values_now, keys_base, values_base, codes):
    heads = 4
    wide = pl.BlockSpec((ROWS, heads * HD), lambda i: (0, i))
    return pl.pallas_call(
        functools.partial(pack_kernel, heads),
        grid=(HEADS // heads,),
        in_specs=[wide] * 5 + [pl.BlockSpec((ROWS, 2 * HEADS), lambda i: (0, 0))],
        out_specs=pl.BlockSpec((heads, 3 * ROWS, HD), lambda i: (i, 0, 0)),
        out_shape=jax.ShapeDtypeStruct((HEADS, 3 * ROWS, HD), bf16),
        compiler_params=pltpu.CompilerParams(vmem_limit_bytes=60 * 2**20),
        name="pack",
    )(queries, keys_now, values_now, keys_base, values_base, codes)


def lay_out(rec_ref, k_ref, vt_ref):
    group = 16
    count = group * ROWS

    def step(g, carry):
        part = rec_ref[pl.ds(g * group, group)].astype(f32)
        keys = part[:, 0:ROWS].reshape(count, HD)
        values = part[:, ROWS : 2 * ROWS].reshape(count, HD)
        start = pl.multiple_of(g * count, HD)
        k_ref[pl.ds(start, count), :] = keys.astype(bf16)
        vt_ref[0:HD, pl.ds(start, count)] = values.T.astype(bf16)
        return carry

    lax.fori_loop(0, HEADS // group, step, 0)
    vt_ref[HD : HD + SUMS, :] = jnp.ones((SUMS, KV), bf16)


def scale_queries(chunk):
    rows = chunk.reshape(BQ, HD) * LOGIT
    high = rows.astype(bf16)
    low = (rows - high.astype(f32)).astype(bf16)
    return jnp.concatenate([high, low], axis=1)


def attention(q, sets, held, store):
    per_set = KV // BK
    blocks = len(sets) * per_set

    def keys_at(k_ref, j):
        if isinstance(j, int):
            return k_ref[j * BK : (j + 1) * BK, :]
        return k_ref[pl.ds(pl.multiple_of(j * BK, BK), BK), :]

    def values_at(vt_ref, j):
        if isinstance(j, int):
            return vt_ref[:, j * BK : (j + 1) * BK]
        return vt_ref[:, pl.ds(pl.multiple_of(j * BK, BK), BK)]

    def scores(k_ref, j):
        k = keys_at(k_ref, j)
        k = jnp.concatenate([k, k], axis=1)
        return lax.dot_general(k, q, (((1,), (1,)), ((), ())), preferred_element_type=f32)

    def weigh(vt_ref, j, s, shift):
        weights = jnp.exp2(s - shift).astype(bf16)
        return jnp.dot(values_at(vt_ref, j), weights, preferred_element_type=f32)

    order = [(k_ref, vt_ref, j) for k_ref, vt_ref in sets for j in range(per_set)]
    s = scores(order[0][0], order[0][2])
    shift = jnp.max(s, axis=0, keepdims=True) if held is None else held[0]
    total = None if held is None else held[1]
    largest = shift
    for n, (_, vt_ref, j) in enumerate(order):
        coming = scores(order[n + 1][0], order[n + 1][2]) if n + 1 < blocks else None
        if n or held is not None:
            largest = jnp.maximum(largest, jnp.max(s, axis=0, keepdims=True))
        part = weigh(vt_ref, j, s, shift)
        total = part if total is None else total + part
        s = coming
    store(shift, total)

    @pl.when(jnp.max(largest - shift) > SLACK)
    def _():
        if held is None:
            state = (jnp.full((1, BQ), -jnp.inf, f32), jnp.zeros((HD + SUMS, BQ), f32))
        else:
            state = held
        for k_ref, vt_ref in sets:

            def step(j, state, k_ref=k_ref, vt_ref=vt_ref):
                top, total = state
                s = scores(k_ref, j)
                newer = jnp.maximum(top, jnp.max(s, axis=0, keepdims=True))
                return newer, total * jnp.exp2(top - newer) + weigh(vt_ref, j, s, newer)

            state = lax.fori_loop(0, per_set, step, state)
        store(*state)


def own_kernel(from_row, lays_out, *refs):
    if lays_out:
        rec_ref, k_ref, vt_ref, *refs = refs
        lay_out(rec_ref, k_ref, vt_ref)
    else:
        rec_ref, k_ref, vt_ref, *refs = refs
    chunks = len(refs) // 3
    q_refs, shift_refs, total_refs = (refs[n * chunks : (n + 1) * chunks] for n in range(3))
    queries = rec_ref[:, 2 * ROWS : 3 * ROWS].astype(f32)
    for b in range(chunks):
        at = from_row + b * CROWS
        q_refs[b][...] = scale_queries(queries[:, at : at + CROWS])
    for b in range(chunks):

        def store(shift, total, b=b):
            shift_refs[b][...] = jnp.broadcast_to(shift, (8, BQ))
            total_refs[b][...] = total

        attention(q_refs[b][...], [(k_ref, vt_ref)], None, store)


def partner_kernel(from_row, lays_out, q_ref, k0_ref, vt0_ref, *refs):
    q = scale_queries(q_ref[:, from_row : from_row + CROWS].astype(f32))
    if lays_out:
        rec_ref, out_ref, k1_ref, vt1_ref = refs
        lay_out(rec_ref, k1_ref, vt1_ref)
    else:
        k1_ref, vt1_ref, out_ref = refs

    def store(shift, total):
        sums = total[HD : HD + 1]
        out_ref[0:HD, :] = (total[:HD] / sums).astype(bf16)
        log = shift + jnp.log(sums) * 1.4426950408889634
        high = log.astype(bf16).astype(f32)
        middle = (log - high).astype(bf16).astype(f32)
        low = log - high - middle
        rows = [high, middle, low, jnp.zeros((SUMS - 3, BQ), f32)]
        out_ref[HD : HD + SUMS, :] = jnp.concatenate(rows, axis=0).astype(bf16)

    attention(q, [(k0_ref, vt0_ref), (k1_ref, vt1_ref)], None, store)


def last_kernel(q_ref, k_ref, vt_ref, shift_ref, total_ref, part_ref, out_ref):
    def store(shift, total):
        part = part_ref[...].astype(f32)
        log = part[HD : HD + 1] + part[HD + 1 : HD + 2] + part[HD + 2 : HD + 3]
        top = jnp.maximum(shift, log)
        mine, theirs = jnp.exp2(shift - top), jnp.exp2(log - top)
        sums = total[HD : HD + 1] * mine + theirs
        merged = (total[:HD] * mine + part[:HD] * theirs) / sums
        out_ref[...] = merged.T.reshape(HEADS, CROWS, HD).astype(bf16)

    attention(q_ref[...], [(k_ref, vt_ref)], (shift_ref[0:1], total_ref[...]), store)


VMEM = pl.BlockSpec(memory_space=pltpu.VMEM)
QUERIES = jax.ShapeDtypeStruct((BQ, 2 * HD), bf16)
KEYS = jax.ShapeDtypeStruct((KV, HD), bf16)
VALUES = jax.ShapeDtypeStruct((HD + SUMS, KV), bf16)
SHIFTS = jax.ShapeDtypeStruct((8, BQ), f32)
TOTALS = jax.ShapeDtypeStruct((HD + SUMS, BQ), f32)
PART = jax.ShapeDtypeStruct((HD + SUMS, BQ), bf16)


def attend(kernel, name, outs, scores, *args):
    return pl.pallas_call(
        kernel,
        in_specs=[VMEM] * len(args),
        out_specs=[VMEM] * len(outs),
        out_shape=outs,
        compiler_params=pltpu.CompilerParams(vmem_limit_bytes=24 * 2**20),
        cost_estimate=pl.CostEstimate(
            flops=scores * HD // 4, bytes_accessed=2**16, transcendentals=0
        ),
        name=name,
    )(*args)


def exchange(messages):
    return lax.all_to_all(messages, "space", split_axis=0, concat_axis=0, tiled=True)


def swap(array, axis):
    return lax.ppermute(array, axis, [(0, 1), (1, 0)])


def per_device(queries, keys_now, values_now, keys_base, values_base, scale_codes):
    own = exchange(pack(queries, keys_now, values_now, keys_base, values_base, scale_codes))
    first = 2 * ROWS + CROWS
    near = swap(own[:, 2 * ROWS : first], "yhi")
    other = swap(own, "core")
    per_chunk = [QUERIES, SHIFTS, TOTALS]
    k0, vt0, *held = attend(
        functools.partial(own_kernel, 0, True), "own_first", [KEYS, VALUES] + per_chunk, BQ * KV, own
    )
    own, near, k0 = lax.optimization_barrier((own, near, k0))
    far = swap(own[:, first : 3 * ROWS], "yhi")
    more = attend(
        functools.partial(own_kernel, CROWS, False),
        "own", [spec for spec in per_chunk for _ in range(2)], 2 * BQ * KV, own, k0, vt0,
    )
    near, *more = lax.optimization_barrier((near, *more))
    held = [list(held), more[0::2], more[1::2]]
    part, k1, vt1 = attend(
        functools.partial(partner_kernel, 0, True),
        "partner_first", [PART, KEYS, VALUES], 2 * BQ * KV, near, k0, vt0, other,
    )
    parts = [swap(part, "yhi")]
    for b in range(1, CHUNKS):
        (part,) = attend(
            functools.partial(partner_kernel, (b - 1) * CROWS, False),
            "partner", [PART], 2 * BQ * KV, far, k0, vt0, k1, vt1,
        )
        parts.append(swap(part, "yhi"))
    out = jax.ShapeDtypeStruct((HEADS, CROWS, HD), bf16)
    merged = []
    for b in range(CHUNKS):
        q, shifts, totals = held[b]
        merged += attend(last_kernel, "last", [out], BQ * KV, q, k1, vt1, shifts, totals, parts[b])
        if b + 1 < CHUNKS:
            merged[b], held[b + 1][0] = lax.optimization_barrier((merged[b], held[b + 1][0]))
    done = exchange(jnp.concatenate(merged, axis=1))
    return done.transpose(1, 0, 2).reshape(ROWS, HEADS * HD)


def solution(mesh):
    finer = Mesh(mesh.devices.reshape(HEADS, 2, 2), ("space", "yhi", "core"))
    rows = P(("space", "yhi", "core"), None)
    return jax.shard_map(
        per_device, mesh=finer, in_specs=(rows,) * 6, out_specs=rows, check_vma=False
    )
```

```python
import functools

import jax
import jax.numpy as jnp
from jax import lax
from jax.experimental import pallas as pl
from jax.experimental.pallas import tpu as pltpu
from jax.sharding import Mesh
from jax.sharding import PartitionSpec as P

HEADS = 32
HD = 128
ROWS = 72
SATURATE = 448.0
LOGIT = 128 ** -0.5 * 1.4426950408889634
CUTS = ((0, 32), (32, 56), (56, 72))
QN = HEADS * ROWS
KV = HEADS * ROWS
SUMS = 16
SLACK = 64.0
BK = 768
CAREFUL = 128
f32 = jnp.float32
bf16 = jnp.bfloat16


def pick_columns(first, count, parity):
    row = lax.broadcasted_iota(jnp.int32, (2 * HEADS, count * HD), 0)
    col = lax.broadcasted_iota(jnp.int32, (2 * HEADS, count * HD), 1)
    return (row == 2 * (first + col // HD) + parity).astype(f32).astype(bf16)


def rebuild(now, base, growth, shrink):
    base = base.astype(f32)
    residual = jnp.clip((now.astype(f32) - base) * shrink, -SATURATE, SATURATE)
    return (base + growth * residual.astype(bf16).astype(f32)).astype(bf16).astype(f32)


def pack_kernel(heads, q_ref, kn_ref, vn_ref, kb_ref, vb_ref, code_ref, out_ref):
    first = pl.program_id(0) * heads
    codes = code_ref[...]
    one = jnp.ones_like(codes)
    up = (jnp.left_shift(one, codes + 16).astype(f32) * (1.0 / 65536.0)).astype(bf16)
    down = jnp.left_shift(one, -codes).astype(f32).astype(bf16)
    down_rows = (((0,), (0,)), ((), ()))
    made = []
    for parity, now_ref, base_ref in ((0, kn_ref, kb_ref), (1, vn_ref, vb_ref)):
        pick = pick_columns(first, heads, parity)
        growth = lax.dot_general(up, pick, down_rows, preferred_element_type=f32)
        shrink = lax.dot_general(down, pick, down_rows, preferred_element_type=f32)
        made.append(rebuild(now_ref[...], base_ref[...], growth, shrink))
    keys, values = made
    queries = q_ref[...].astype(f32)
    for h in range(heads):
        cols = slice(h * HD, (h + 1) * HD)
        message = [keys[:, cols], values[:, cols], queries[:, cols]]
        out_ref[h] = jnp.concatenate(message, axis=0).astype(bf16)


def pack(queries, keys_now, values_now, keys_base, values_base, codes):
    heads = 8
    wide = pl.BlockSpec((ROWS, heads * HD), lambda i: (0, i))
    return pl.pallas_call(
        functools.partial(pack_kernel, heads),
        grid=(HEADS // heads,),
        in_specs=[wide] * 5 + [pl.BlockSpec((2 * HEADS, ROWS), lambda i: (0, 0))],
        out_specs=pl.BlockSpec((heads, 3 * ROWS, HD), lambda i: (i, 0, 0)),
        out_shape=jax.ShapeDtypeStruct((HEADS, 3 * ROWS, HD), bf16),
        compiler_params=pltpu.CompilerParams(vmem_limit_bytes=60 * 2**20),
        name="pack",
    )(queries, keys_now, values_now, keys_base, values_base, codes.T)


def lay_out(rec_ref, k_ref, vt_ref):
    group = 16
    count = group * ROWS

    def step(g, carry):
        part = rec_ref[pl.ds(g * group, group)].astype(f32)
        keys = part[:, 0:ROWS].reshape(count, HD)
        values = part[:, ROWS : 2 * ROWS].reshape(count, HD)
        start = pl.multiple_of(g * count, HD)
        k_ref[pl.ds(start, count), :] = keys.astype(bf16)
        vt_ref[0:HD, pl.ds(start, count)] = values.T.astype(bf16)
        return carry

    lax.fori_loop(0, HEADS // group, step, 0)
    vt_ref[HD : HD + SUMS, :] = jnp.ones((SUMS, KV), bf16)


def scale_queries(chunk):
    rows = chunk.reshape(HEADS * chunk.shape[1], HD) * LOGIT
    high = rows.astype(bf16)
    low = (rows - high.astype(f32)).astype(bf16)
    return jnp.concatenate([high, low], axis=1)


def attention(q, sets, held, store):
    def scores(k_ref, block):
        k = k_ref[block, :]
        k = jnp.concatenate([k, k], axis=1)
        return lax.dot_general(k, q, (((1,), (1,)), ((), ())), preferred_element_type=f32)

    def weigh(vt_ref, block, s, shift):
        weights = jnp.exp2(s - shift).astype(bf16)
        return jnp.dot(vt_ref[:, block], weights, preferred_element_type=f32)

    order = [
        (k_ref, vt_ref, slice(at, at + BK)) for k_ref, vt_ref in sets for at in range(0, KV, BK)
    ]
    blocks = len(order)
    s = scores(order[0][0], order[0][2])
    shift = jnp.max(s, axis=0, keepdims=True) if held is None else held[0]
    total = None if held is None else held[1]
    largest = shift
    for n, (_, vt_ref, block) in enumerate(order):
        coming = scores(order[n + 1][0], order[n + 1][2]) if n + 1 < blocks else None
        if n or held is not None:
            largest = jnp.maximum(largest, jnp.max(s, axis=0, keepdims=True))
        part = weigh(vt_ref, block, s, shift)
        total = part if total is None else total + part
        s = coming
    store(shift, total)

    @pl.when(jnp.max(largest - shift) > SLACK)
    def _():
        if held is None:
            state = (jnp.full(shift.shape, -jnp.inf, f32), jnp.zeros(total.shape, f32))
        else:
            state = held
        for k_ref, vt_ref in sets:

            def step(j, state, k_ref=k_ref, vt_ref=vt_ref):
                top, total = state
                block = pl.ds(pl.multiple_of(j * CAREFUL, CAREFUL), CAREFUL)
                s = scores(k_ref, block)
                newer = jnp.maximum(top, jnp.max(s, axis=0, keepdims=True))
                return newer, total * jnp.exp2(top - newer) + weigh(vt_ref, block, s, newer)

            state = lax.fori_loop(0, KV // CAREFUL, step, state)
        store(*state)


def own_kernel(rec_ref, k_ref, vt_ref, *refs):
    lay_out(rec_ref, k_ref, vt_ref)
    count = len(CUTS)
    q_refs, shift_refs, total_refs = (refs[n * count : (n + 1) * count] for n in range(3))
    queries = rec_ref[:, 2 * ROWS : 3 * ROWS].astype(f32)
    for n, (top, end) in enumerate(CUTS):
        q_refs[n][...] = scale_queries(queries[:, top:end])
    for n in range(count):

        def store(shift, total, n=n):
            shift_refs[n][...] = jnp.broadcast_to(shift, shift_refs[n].shape)
            total_refs[n][...] = total

        attention(q_refs[n][...], [(k_ref, vt_ref)], None, store)


def partner_kernel(lays_out, q_ref, k0_ref, vt0_ref, *refs):
    if lays_out:
        rec_ref, out_ref, k1_ref, vt1_ref = refs
        lay_out(rec_ref, k1_ref, vt1_ref)
    else:
        k1_ref, vt1_ref, out_ref = refs

    def store(shift, total):
        sums = total[HD : HD + 1]
        out_ref[0:HD, :] = (total[:HD] / sums).astype(bf16)
        log = shift + jnp.log(sums) * 1.4426950408889634
        high = log.astype(bf16).astype(f32)
        middle = (log - high).astype(bf16).astype(f32)
        low = log - high - middle
        rows = [high, middle, low, jnp.zeros((SUMS - 3, log.shape[1]), f32)]
        out_ref[HD : HD + SUMS, :] = jnp.concatenate(rows, axis=0).astype(bf16)

    q = scale_queries(q_ref[...].astype(f32))
    attention(q, [(k0_ref, vt0_ref), (k1_ref, vt1_ref)], None, store)


def merge(shift, total, part_ref, out_ref):
    part = part_ref[...].astype(f32)
    log = part[HD : HD + 1] + part[HD + 1 : HD + 2] + part[HD + 2 : HD + 3]
    top = jnp.maximum(shift, log)
    mine, theirs = jnp.exp2(shift - top), jnp.exp2(log - top)
    sums = total[HD : HD + 1] * mine + theirs
    merged = (total[:HD] * mine + part[:HD] * theirs) / sums
    out_ref[...] = merged.T.reshape(out_ref.shape).astype(bf16)


def last_kernel(q_ref, k_ref, vt_ref, shift_ref, total_ref, part_ref, out_ref):
    def store(shift, total):
        merge(shift, total, part_ref, out_ref)

    attention(q_ref[...], [(k_ref, vt_ref)], (shift_ref[0:1], total_ref[...]), store)


def other_kernel(q_ref, k_ref, vt_ref, shift_ref, total_ref, next_shift, next_total):
    def store(shift, total):
        next_shift[...] = jnp.broadcast_to(shift, next_shift.shape)
        next_total[...] = total

    attention(q_ref[...], [(k_ref, vt_ref)], (shift_ref[0:1], total_ref[...]), store)


def merge_kernel(shift_ref, total_ref, part_ref, out_ref):
    merge(shift_ref[0:1], total_ref[...], part_ref, out_ref)


VMEM = pl.BlockSpec(memory_space=pltpu.VMEM)
SIZES = [HEADS * (end - top) for top, end in CUTS]
QUERIES = [jax.ShapeDtypeStruct((n, 2 * HD), bf16) for n in SIZES]
KEYS = jax.ShapeDtypeStruct((KV, HD), bf16)
VALUES = jax.ShapeDtypeStruct((HD + SUMS, KV), bf16)
SHIFTS = [jax.ShapeDtypeStruct((8, n), f32) for n in SIZES]
TOTALS = [jax.ShapeDtypeStruct((HD + SUMS, n), f32) for n in SIZES]
PARTS = [jax.ShapeDtypeStruct((HD + SUMS, n), bf16) for n in SIZES]
OUTS = [jax.ShapeDtypeStruct((HEADS, end - top, HD), bf16) for top, end in CUTS]


def attend(kernel, name, outs, *args):
    return pl.pallas_call(
        kernel,
        in_specs=[VMEM] * len(args),
        out_specs=[VMEM] * len(outs),
        out_shape=outs,
        compiler_params=pltpu.CompilerParams(vmem_limit_bytes=24 * 2**20),
        cost_estimate=pl.CostEstimate(flops=0, bytes_accessed=0, transcendentals=0),
        name=name,
    )(*args)


def exchange(messages):
    return lax.all_to_all(messages, "space", split_axis=0, concat_axis=0, tiled=True)


def swap(array, axis):
    return lax.ppermute(array, axis, [(0, 1), (1, 0)])


def per_device(queries, keys_now, values_now, keys_base, values_base, scale_codes):
    own = exchange(pack(queries, keys_now, values_now, keys_base, values_base, scale_codes))
    theirs = [swap(own[:, 2 * ROWS + top : 2 * ROWS + end], "yhi") for top, end in CUTS]
    other = swap(own, "core")
    count = len(CUTS)
    k0, vt0, *held = attend(own_kernel, "own", [KEYS, VALUES] + QUERIES + SHIFTS + TOTALS, own)
    held = [held[n::count] for n in range(count)]
    part, k1, vt1 = attend(
        functools.partial(partner_kernel, True),
        "partner_first", [PARTS[0], KEYS, VALUES], theirs[0], k0, vt0, other,
    )
    parts = [swap(part, "yhi")]
    for n in range(1, count):
        (part,) = attend(
            functools.partial(partner_kernel, False),
            "partner", [PARTS[n]], theirs[n], k0, vt0, k1, vt1,
        )
        parts.append(swap(part, "yhi"))
    merged = []
    for n in range(count):
        q, shift, total = held[n]
        if n + 1 < count:
            merged += attend(last_kernel, "last", [OUTS[n]], q, k1, vt1, shift, total, parts[n])
            merged[n], held[n + 1][0] = lax.optimization_barrier((merged[n], held[n + 1][0]))
        else:
            shift, total = attend(
                other_kernel, "other", [SHIFTS[n], TOTALS[n]], q, k1, vt1, shift, total
            )
            merged += attend(merge_kernel, "merge", [OUTS[n]], shift, total, parts[n])
    done = exchange(jnp.concatenate(merged, axis=1))
    return done.transpose(1, 0, 2).reshape(ROWS, HEADS * HD)


def solution(mesh):
    finer = Mesh(mesh.devices.reshape(HEADS, 2, 2), ("space", "yhi", "core"))
    rows = P(("space", "yhi", "core"), None)
    return jax.shard_map(
        per_device, mesh=finer, in_specs=(rows,) * 6, out_specs=rows, check_vma=False
    )
```

```python
import functools
import itertools

import jax
import jax.numpy as jnp
from jax import lax
from jax.experimental import pallas as pl
from jax.experimental.pallas import tpu as pltpu
from jax.sharding import Mesh
from jax.sharding import PartitionSpec as P

HEADS = 32
HD = 128
ROWS = 72
SATURATE = 448.0
LOGIT = 128 ** -0.5 * 1.4426950408889634
CUTS = ((0, 32), (32, 56), (56, 72))
QN = HEADS * ROWS
KV = HEADS * ROWS
SUMS = 16
SLACK = 64.0
STEPS = {1: ((256, 1024, 768, 256),), 2: ((256, 1024, 1024), (1024, 1024, 256))}
CAREFUL = 128
f32 = jnp.float32
bf16 = jnp.bfloat16


def pick_columns(first, count, parity):
    row = lax.broadcasted_iota(jnp.int32, (2 * HEADS, count * HD), 0)
    col = lax.broadcasted_iota(jnp.int32, (2 * HEADS, count * HD), 1)
    return (row == 2 * (first + col // HD) + parity).astype(f32).astype(bf16)


def rebuild(now, base, growth, shrink):
    base = base.astype(f32)
    residual = jnp.clip((now.astype(f32) - base) * shrink, -SATURATE, SATURATE)
    return (base + growth * residual.astype(bf16).astype(f32)).astype(bf16).astype(f32)


def pack_kernel(heads, q_ref, kn_ref, vn_ref, kb_ref, vb_ref, code_ref, out_ref):
    first = pl.program_id(0) * heads
    codes = code_ref[...]
    one = jnp.ones_like(codes)
    up = (jnp.left_shift(one, codes + 16).astype(f32) * (1.0 / 65536.0)).astype(bf16)
    down = jnp.left_shift(one, -codes).astype(f32).astype(bf16)
    down_rows = (((0,), (0,)), ((), ()))
    made = []
    for parity, now_ref, base_ref in ((0, kn_ref, kb_ref), (1, vn_ref, vb_ref)):
        pick = pick_columns(first, heads, parity)
        growth = lax.dot_general(up, pick, down_rows, preferred_element_type=f32)
        shrink = lax.dot_general(down, pick, down_rows, preferred_element_type=f32)
        made.append(rebuild(now_ref[...], base_ref[...], growth, shrink))
    keys, values = made
    queries = q_ref[...].astype(f32)
    for h in range(heads):
        cols = slice(h * HD, (h + 1) * HD)
        message = [keys[:, cols], values[:, cols], queries[:, cols]]
        out_ref[h] = jnp.concatenate(message, axis=0).astype(bf16)


def pack(queries, keys_now, values_now, keys_base, values_base, codes):
    heads = 16
    wide = pl.BlockSpec((ROWS, heads * HD), lambda i: (0, i))
    return pl.pallas_call(
        functools.partial(pack_kernel, heads),
        grid=(HEADS // heads,),
        in_specs=[wide] * 5 + [pl.BlockSpec((2 * HEADS, ROWS), lambda i: (0, 0))],
        out_specs=pl.BlockSpec((heads, 3 * ROWS, HD), lambda i: (i, 0, 0)),
        out_shape=jax.ShapeDtypeStruct((HEADS, 3 * ROWS, HD), bf16),
        compiler_params=pltpu.CompilerParams(vmem_limit_bytes=60 * 2**20),
        name="pack",
    )(queries, keys_now, values_now, keys_base, values_base, codes.T)


def lay_out(rec_ref, k_ref, vt_ref):
    group = 16
    count = group * ROWS

    def step(g, carry):
        part = rec_ref[pl.ds(g * group, group)].astype(f32)
        keys = part[:, 0:ROWS].reshape(count, HD)
        values = part[:, ROWS : 2 * ROWS].reshape(count, HD)
        start = pl.multiple_of(g * count, HD)
        k_ref[pl.ds(start, count), :] = keys.astype(bf16)
        vt_ref[0:HD, pl.ds(start, count)] = values.T.astype(bf16)
        return carry

    lax.fori_loop(0, HEADS // group, step, 0)
    vt_ref[HD : HD + SUMS, :] = jnp.ones((SUMS, KV), bf16)


def scale_queries(chunk):
    rows = chunk.reshape(HEADS * chunk.shape[1], HD) * LOGIT
    high = rows.astype(bf16)
    low = (rows - high.astype(f32)).astype(bf16)
    return jnp.concatenate([high, low], axis=1)


def attention(q, sets, held, store):
    def scores(k_ref, block):
        k = k_ref[block, :]
        k = jnp.concatenate([k, k], axis=1)
        return lax.dot_general(k, q, (((1,), (1,)), ((), ())), preferred_element_type=f32)

    def weigh(vt_ref, block, s, shift):
        weights = jnp.exp2(s - shift).astype(bf16)
        return jnp.dot(vt_ref[:, block], weights, preferred_element_type=f32)

    order = []
    for (k_ref, vt_ref), steps in zip(sets, STEPS[len(sets)]):
        for at, step in zip(itertools.accumulate(steps, initial=0), steps):
            order.append((k_ref, vt_ref, slice(at, at + step)))
    blocks = len(order)
    s = scores(order[0][0], order[0][2])
    shift = jnp.max(s, axis=0, keepdims=True) if held is None else held[0]
    total = None if held is None else held[1]
    largest = shift
    for n, (_, vt_ref, block) in enumerate(order):
        coming = scores(order[n + 1][0], order[n + 1][2]) if n + 1 < blocks else None
        if n or held is not None:
            largest = jnp.maximum(largest, jnp.max(s, axis=0, keepdims=True))
        part = weigh(vt_ref, block, s, shift)
        total = part if total is None else total + part
        s = coming
    store(shift, total)

    @pl.when(jnp.max(largest - shift) > SLACK)
    def _():
        if held is None:
            state = (jnp.full(shift.shape, -jnp.inf, f32), jnp.zeros(total.shape, f32))
        else:
            state = held
        for k_ref, vt_ref in sets:

            def step(j, state, k_ref=k_ref, vt_ref=vt_ref):
                top, total = state
                block = pl.ds(pl.multiple_of(j * CAREFUL, CAREFUL), CAREFUL)
                s = scores(k_ref, block)
                newer = jnp.maximum(top, jnp.max(s, axis=0, keepdims=True))
                return newer, total * jnp.exp2(top - newer) + weigh(vt_ref, block, s, newer)

            state = lax.fori_loop(0, KV // CAREFUL, step, state)
        store(*state)


def own_kernel(rec_ref, k_ref, vt_ref, *refs):
    lay_out(rec_ref, k_ref, vt_ref)
    count = len(CUTS)
    q_refs, shift_refs, total_refs = (refs[n * count : (n + 1) * count] for n in range(3))
    queries = rec_ref[:, 2 * ROWS : 3 * ROWS].astype(f32)
    for n, (top, end) in enumerate(CUTS):
        q_refs[n][...] = scale_queries(queries[:, top:end])
    for n in range(count):

        def store(shift, total, n=n):
            shift_refs[n][...] = jnp.broadcast_to(shift, shift_refs[n].shape)
            total_refs[n][...] = total

        attention(q_refs[n][...], [(k_ref, vt_ref)], None, store)


def partner_kernel(lays_out, q_ref, k0_ref, vt0_ref, *refs):
    if lays_out:
        rec_ref, out_ref, k1_ref, vt1_ref = refs
        lay_out(rec_ref, k1_ref, vt1_ref)
    else:
        k1_ref, vt1_ref, out_ref = refs

    def store(shift, total):
        sums = total[HD : HD + 1]
        out_ref[0:HD, :] = (total[:HD] * (1.0 / sums)).astype(bf16)
        log = shift + jnp.log(sums) * 1.4426950408889634
        high = log.astype(bf16).astype(f32)
        middle = (log - high).astype(bf16).astype(f32)
        low = log - high - middle
        rows = [high, middle, low, jnp.zeros((SUMS - 3, log.shape[1]), f32)]
        out_ref[HD : HD + SUMS, :] = jnp.concatenate(rows, axis=0).astype(bf16)

    q = scale_queries(q_ref[...].astype(f32))
    attention(q, [(k0_ref, vt0_ref), (k1_ref, vt1_ref)], None, store)


def merge(shift, total, part_ref, out_ref):
    part = part_ref[...].astype(f32)
    log = part[HD : HD + 1] + part[HD + 1 : HD + 2] + part[HD + 2 : HD + 3]
    top = jnp.maximum(shift, log)
    mine, theirs = jnp.exp2(shift - top), jnp.exp2(log - top)
    sums = total[HD : HD + 1] * mine + theirs
    merged = total[:HD] * (mine / sums) + part[:HD] * (theirs / sums)
    out_ref[...] = merged.T.reshape(out_ref.shape).astype(bf16)


def last_kernel(q_ref, k_ref, vt_ref, shift_ref, total_ref, part_ref, out_ref):
    def store(shift, total):
        merge(shift, total, part_ref, out_ref)

    attention(q_ref[...], [(k_ref, vt_ref)], (shift_ref[0:1], total_ref[...]), store)


def other_kernel(q_ref, k_ref, vt_ref, shift_ref, total_ref, next_shift, next_total):
    def store(shift, total):
        next_shift[...] = jnp.broadcast_to(shift, next_shift.shape)
        next_total[...] = total

    attention(q_ref[...], [(k_ref, vt_ref)], (shift_ref[0:1], total_ref[...]), store)


def merge_kernel(shift_ref, total_ref, part_ref, out_ref):
    merge(shift_ref[0:1], total_ref[...], part_ref, out_ref)


VMEM = pl.BlockSpec(memory_space=pltpu.VMEM)
SIZES = [HEADS * (end - top) for top, end in CUTS]
QUERIES = [jax.ShapeDtypeStruct((n, 2 * HD), bf16) for n in SIZES]
KEYS = jax.ShapeDtypeStruct((KV, HD), bf16)
VALUES = jax.ShapeDtypeStruct((HD + SUMS, KV), bf16)
SHIFTS = [jax.ShapeDtypeStruct((8, n), f32) for n in SIZES]
TOTALS = [jax.ShapeDtypeStruct((HD + SUMS, n), f32) for n in SIZES]
PARTS = [jax.ShapeDtypeStruct((HD + SUMS, n), bf16) for n in SIZES]
OUTS = [jax.ShapeDtypeStruct((HEADS, end - top, HD), bf16) for top, end in CUTS]


def attend(kernel, name, outs, *args):
    return pl.pallas_call(
        kernel,
        in_specs=[VMEM] * len(args),
        out_specs=[VMEM] * len(outs),
        out_shape=outs,
        compiler_params=pltpu.CompilerParams(vmem_limit_bytes=24 * 2**20),
        cost_estimate=pl.CostEstimate(flops=0, bytes_accessed=0, transcendentals=0),
        name=name,
    )(*args)


def device(x, ylo, z, yhi, core):
    return (((x * 2 + ylo) * 4 + z) * 2 + yhi) * 2 + core


GROUPS = [
    [
        device(x, side ^ yhi, z, yhi, core)
        for x, z, yhi in itertools.product(range(4), range(4), range(2))
    ]
    for side, core in itertools.product(range(2), range(2))
]
PAIRS = {"chip": [], "core": []}
for x, ylo, z, yhi, core in itertools.product(range(4), range(2), range(4), range(2), range(2)):
    here = device(x, ylo, z, yhi, core)
    PAIRS["chip"].append((here, device(x, 1 - ylo, z, yhi, core)))
    PAIRS["core"].append((here, device(x, ylo, z, yhi, 1 - core)))


def exchange(messages):
    return lax.all_to_all(
        messages, "device", split_axis=0, concat_axis=0, axis_index_groups=GROUPS, tiled=True
    )


def swap(array, which):
    return lax.ppermute(array, "device", PAIRS[which])


def per_device(queries, keys_now, values_now, keys_base, values_base, scale_codes):
    own = exchange(pack(queries, keys_now, values_now, keys_base, values_base, scale_codes))
    theirs = [swap(own[:, 2 * ROWS + top : 2 * ROWS + end], "chip") for top, end in CUTS]
    theirs[1:] = lax.optimization_barrier(theirs[1:])
    other = swap(own, "core")
    count = len(CUTS)
    k0, vt0, *held = attend(own_kernel, "own", [KEYS, VALUES] + QUERIES + SHIFTS + TOTALS, own)
    held = [held[n::count] for n in range(count)]
    part, k1, vt1 = attend(
        functools.partial(partner_kernel, True),
        "partner_first", [PARTS[0], KEYS, VALUES], theirs[0], k0, vt0, other,
    )
    parts = [swap(part, "chip")]
    for n in range(1, count):
        (part,) = attend(
            functools.partial(partner_kernel, False),
            "partner", [PARTS[n]], theirs[n], k0, vt0, k1, vt1,
        )
        parts.append(swap(part, "chip"))
    merged = []
    for n in range(count):
        q, shift, total = held[n]
        if n + 1 < count:
            merged += attend(last_kernel, "last", [OUTS[n]], q, k1, vt1, shift, total, parts[n])
            merged[n], held[n + 1][0] = lax.optimization_barrier((merged[n], held[n + 1][0]))
        else:
            shift, total = attend(
                other_kernel, "other", [SHIFTS[n], TOTALS[n]], q, k1, vt1, shift, total
            )
            merged += attend(merge_kernel, "merge", [OUTS[n]], shift, total, parts[n])
    done = exchange(jnp.concatenate(merged, axis=1))
    return done.transpose(1, 0, 2).reshape(ROWS, HEADS * HD)


def solution(mesh):
    flat = Mesh(mesh.devices.reshape(-1), ("device",))
    rows = P("device", None)
    return jax.shard_map(
        per_device, mesh=flat, in_specs=(rows,) * 6, out_specs=rows, check_vma=False
    )
```

```python
import functools
import itertools

import jax
import jax.numpy as jnp
from jax import lax
from jax.experimental import pallas as pl
from jax.experimental.pallas import tpu as pltpu
from jax.sharding import Mesh
from jax.sharding import PartitionSpec as P

HEADS = 32
HD = 128
ROWS = 72
SATURATE = 448.0
LOGIT = 128 ** -0.5 * 1.4426950408889634
CUTS = ((0, 32), (32, 56), (56, 72))
QN = HEADS * ROWS
KV = HEADS * ROWS
SUMS = 16
LOGS = 8
SLACK = 64.0
STEPS = {1: ((256, 1024, 768, 256),), 2: ((256, 1024, 1024), (1024, 1024, 256))}
CAREFUL = 128
f32 = jnp.float32
bf16 = jnp.bfloat16


def pick_columns(first, count, parity):
    row = lax.broadcasted_iota(jnp.int32, (2 * HEADS, count * HD), 0)
    col = lax.broadcasted_iota(jnp.int32, (2 * HEADS, count * HD), 1)
    return (row == 2 * (first + col // HD) + parity).astype(f32).astype(bf16)


def rebuild(now, base, limit):
    base = base.astype(f32)
    residual = jnp.clip(now.astype(f32) - base, -limit, limit)
    return (base + residual.astype(bf16).astype(f32)).astype(bf16).astype(f32)


def pack_kernel(heads, q_ref, kn_ref, vn_ref, kb_ref, vb_ref, code_ref, out_ref):
    first = pl.program_id(0) * heads
    codes = code_ref[...]
    steps = jnp.left_shift(jnp.ones_like(codes), codes + 16).astype(f32)
    limits = (steps * (SATURATE / 65536.0)).astype(bf16)
    made = []
    for parity, now_ref, base_ref in ((0, kn_ref, kb_ref), (1, vn_ref, vb_ref)):
        pick = pick_columns(first, heads, parity)
        limit = lax.dot_general(limits, pick, (((0,), (0,)), ((), ())), preferred_element_type=f32)
        made.append(rebuild(now_ref[...], base_ref[...], limit))
    made.append(q_ref[...].astype(f32))
    for h in range(heads):
        message = [part[:, h * HD : (h + 1) * HD] for part in made]
        out_ref[h] = jnp.concatenate(message, axis=0).astype(bf16)


def pack(queries, keys_now, values_now, keys_base, values_base, codes):
    heads = 16
    wide = pl.BlockSpec((ROWS, heads * HD), lambda i: (0, i))
    return pl.pallas_call(
        functools.partial(pack_kernel, heads),
        grid=(HEADS // heads,),
        in_specs=[wide] * 5 + [pl.BlockSpec((2 * HEADS, ROWS), lambda i: (0, 0))],
        out_specs=pl.BlockSpec((heads, 3 * ROWS, HD), lambda i: (i, 0, 0)),
        out_shape=jax.ShapeDtypeStruct((HEADS, 3 * ROWS, HD), bf16),
        compiler_params=pltpu.CompilerParams(vmem_limit_bytes=60 * 2**20),
        name="pack",
    )(queries, keys_now, values_now, keys_base, values_base, codes.T)


def lay_out(rec_ref, k_ref, vt_ref):
    group = 16
    count = group * ROWS
    for g in range(HEADS // group):
        part = rec_ref[g * group : (g + 1) * group].astype(f32)
        keys = part[:, 0:ROWS].reshape(count, HD)
        values = part[:, ROWS : 2 * ROWS].reshape(count, HD)
        k_ref[g * count : (g + 1) * count, :] = keys.astype(bf16)
        vt_ref[0:HD, g * count : (g + 1) * count] = values.T.astype(bf16)
    vt_ref[HD : HD + SUMS, :] = jnp.ones((SUMS, KV), bf16)


def scale_queries(chunk):
    rows = chunk.reshape(HEADS * chunk.shape[1], HD) * LOGIT
    high = rows.astype(bf16)
    low = (rows - high.astype(f32)).astype(bf16)
    return jnp.concatenate([high, low], axis=1)


def attention(q, sets, held, store):
    def scores(k_ref, block):
        k = k_ref[block, :]
        k = jnp.concatenate([k, k], axis=1)
        return lax.dot_general(k, q, (((1,), (1,)), ((), ())), preferred_element_type=f32)

    def weigh(vt_ref, block, s, shift):
        weights = jnp.exp2(s - shift).astype(bf16)
        return jnp.dot(vt_ref[:, block], weights, preferred_element_type=f32)

    order = []
    for (k_ref, vt_ref), steps in zip(sets, STEPS[len(sets)]):
        for at, step in zip(itertools.accumulate(steps, initial=0), steps):
            order.append((k_ref, vt_ref, slice(at, at + step)))
    blocks = len(order)
    s = scores(order[0][0], order[0][2])
    shift = jnp.max(s, axis=0, keepdims=True) if held is None else held[0]
    total = None if held is None else held[1]
    largest = shift
    for n, (_, vt_ref, block) in enumerate(order):
        coming = scores(order[n + 1][0], order[n + 1][2]) if n + 1 < blocks else None
        if n or held is not None:
            largest = jnp.maximum(largest, jnp.max(s, axis=0, keepdims=True))
        part = weigh(vt_ref, block, s, shift)
        total = part if total is None else total + part
        s = coming
    store(shift, total)

    @pl.when(jnp.max(largest - shift) > SLACK)
    def _():
        if held is None:
            state = (jnp.full(shift.shape, -jnp.inf, f32), jnp.zeros(total.shape, f32))
        else:
            state = held
        for k_ref, vt_ref in sets:

            def step(j, state, k_ref=k_ref, vt_ref=vt_ref):
                top, total = state
                block = pl.ds(pl.multiple_of(j * CAREFUL, CAREFUL), CAREFUL)
                s = scores(k_ref, block)
                newer = jnp.maximum(top, jnp.max(s, axis=0, keepdims=True))
                return newer, total * jnp.exp2(top - newer) + weigh(vt_ref, block, s, newer)

            state = lax.fori_loop(0, KV // CAREFUL, step, state)
        store(*state)


def own_kernel(rec_ref, k_ref, vt_ref, *refs):
    lay_out(rec_ref, k_ref, vt_ref)
    count = len(CUTS)
    q_refs, shift_refs, total_refs = (refs[n * count : (n + 1) * count] for n in range(3))
    queries = rec_ref[...].astype(f32)[:, 2 * ROWS : 3 * ROWS]
    for n, (top, end) in enumerate(CUTS):
        q_refs[n][...] = scale_queries(queries[:, top:end])
    for n in range(count):

        def store(shift, total, n=n):
            shift_refs[n][...] = jnp.broadcast_to(shift, shift_refs[n].shape)
            total_refs[n][...] = total

        attention(q_refs[n][...], [(k_ref, vt_ref)], None, store)


def partner_kernel(lays_out, q_ref, k0_ref, vt0_ref, *refs):
    if lays_out:
        rec_ref, out_ref, k1_ref, vt1_ref = refs
        lay_out(rec_ref, k1_ref, vt1_ref)
    else:
        k1_ref, vt1_ref, out_ref = refs

    def store(shift, total):
        sums = total[HD : HD + 1]
        log = shift + jnp.log(sums) * 1.4426950408889634
        high = log.astype(bf16).astype(f32)
        middle = (log - high).astype(bf16).astype(f32)
        low = log - high - middle
        rest = jnp.zeros((LOGS - 3, log.shape[1]), f32)
        rows = [total[:HD] * (1.0 / sums), high, middle, low, rest]
        out_ref[...] = jnp.concatenate(rows, axis=0).astype(bf16)

    q = scale_queries(q_ref[...].astype(f32))
    attention(q, [(k0_ref, vt0_ref), (k1_ref, vt1_ref)], None, store)


def merge(shift, total, part_ref, out_ref):
    part = part_ref[...].astype(f32)
    log = part[HD : HD + 1] + part[HD + 1 : HD + 2] + part[HD + 2 : HD + 3]
    top = jnp.maximum(shift, log)
    mine, theirs = jnp.exp2(shift - top), jnp.exp2(log - top)
    sums = total[HD : HD + 1] * mine + theirs
    merged = total[:HD] * (mine / sums) + part[:HD] * (theirs / sums)
    out_ref[...] = merged.T.reshape(out_ref.shape).astype(bf16)


def last_kernel(q_ref, k_ref, vt_ref, shift_ref, total_ref, part_ref, out_ref):
    def store(shift, total):
        merge(shift, total, part_ref, out_ref)

    attention(q_ref[...], [(k_ref, vt_ref)], (shift_ref[0:1], total_ref[...]), store)


def other_kernel(q_ref, k_ref, vt_ref, shift_ref, total_ref, next_shift, next_total):
    def store(shift, total):
        next_shift[...] = jnp.broadcast_to(shift, next_shift.shape)
        next_total[...] = total

    attention(q_ref[...], [(k_ref, vt_ref)], (shift_ref[0:1], total_ref[...]), store)


def merge_kernel(shift_ref, total_ref, part_ref, out_ref):
    merge(shift_ref[0:1], total_ref[...], part_ref, out_ref)


VMEM = pl.BlockSpec(memory_space=pltpu.VMEM)
SIZES = [HEADS * (end - top) for top, end in CUTS]
QUERIES = [jax.ShapeDtypeStruct((n, 2 * HD), bf16) for n in SIZES]
KEYS = jax.ShapeDtypeStruct((KV, HD), bf16)
VALUES = jax.ShapeDtypeStruct((HD + SUMS, KV), bf16)
SHIFTS = [jax.ShapeDtypeStruct((8, n), f32) for n in SIZES]
TOTALS = [jax.ShapeDtypeStruct((HD + SUMS, n), f32) for n in SIZES]
PARTS = [jax.ShapeDtypeStruct((HD + LOGS, n), bf16) for n in SIZES]
OUTS = [jax.ShapeDtypeStruct((HEADS, end - top, HD), bf16) for top, end in CUTS]


def attend(kernel, name, outs, *args):
    return pl.pallas_call(
        kernel,
        in_specs=[VMEM] * len(args),
        out_specs=[VMEM] * len(outs),
        out_shape=outs,
        compiler_params=pltpu.CompilerParams(vmem_limit_bytes=24 * 2**20),
        cost_estimate=pl.CostEstimate(flops=0, bytes_accessed=0, transcendentals=0),
        name=name,
    )(*args)


def device(x, ylo, z, yhi, core):
    return (((x * 2 + ylo) * 4 + z) * 2 + yhi) * 2 + core


GROUPS = [
    [
        device(x, side ^ yhi, z, yhi, core)
        for x, z, yhi in itertools.product(range(4), range(4), range(2))
    ]
    for side, core in itertools.product(range(2), range(2))
]
PAIRS = {"chip": [], "core": []}
for x, ylo, z, yhi, core in itertools.product(range(4), range(2), range(4), range(2), range(2)):
    here = device(x, ylo, z, yhi, core)
    PAIRS["chip"].append((here, device(x, 1 - ylo, z, yhi, core)))
    PAIRS["core"].append((here, device(x, ylo, z, yhi, 1 - core)))


def exchange(messages):
    return lax.all_to_all(
        messages, "device", split_axis=0, concat_axis=0, axis_index_groups=GROUPS, tiled=True
    )


def swap(array, which):
    return lax.ppermute(array, "device", PAIRS[which])


def per_device(queries, keys_now, values_now, keys_base, values_base, scale_codes):
    own = exchange(pack(queries, keys_now, values_now, keys_base, values_base, scale_codes))
    theirs = [swap(own[:, 2 * ROWS + top : 2 * ROWS + end], "chip") for top, end in CUTS]
    theirs[1:] = lax.optimization_barrier(theirs[1:])
    other = swap(own, "core")
    count = len(CUTS)
    k0, vt0, *held = attend(own_kernel, "own", [KEYS, VALUES] + QUERIES + SHIFTS + TOTALS, own)
    held = [held[n::count] for n in range(count)]
    part, k1, vt1 = attend(
        functools.partial(partner_kernel, True),
        "partner_first", [PARTS[0], KEYS, VALUES], theirs[0], k0, vt0, other,
    )
    parts = [swap(part, "chip")]
    for n in range(1, count):
        (part,) = attend(
            functools.partial(partner_kernel, False),
            "partner", [PARTS[n]], theirs[n], k0, vt0, k1, vt1,
        )
        parts.append(swap(part, "chip"))
    merged = []
    for n in range(count):
        q, shift, total = held[n]
        if n + 1 < count:
            merged += attend(last_kernel, "last", [OUTS[n]], q, k1, vt1, shift, total, parts[n])
            merged[n], held[n + 1][0] = lax.optimization_barrier((merged[n], held[n + 1][0]))
        else:
            shift, total = attend(
                other_kernel, "other", [SHIFTS[n], TOTALS[n]], q, k1, vt1, shift, total
            )
            merged += attend(merge_kernel, "merge", [OUTS[n]], shift, total, parts[n])
    done = exchange(jnp.concatenate(merged, axis=1))
    return done.transpose(1, 0, 2).reshape(ROWS, HEADS * HD)


def solution(mesh):
    flat = Mesh(mesh.devices.reshape(-1), ("device",))
    rows = P("device", None)
    return jax.shard_map(
        per_device, mesh=flat, in_specs=(rows,) * 6, out_specs=rows, check_vma=False
    )
```

```python
import functools
import itertools

import jax
import jax.numpy as jnp
from jax import lax
from jax.experimental import pallas as pl
from jax.experimental.pallas import tpu as pltpu
from jax.sharding import Mesh
from jax.sharding import PartitionSpec as P

HEADS = 32
HD = 128
ROWS = 72
SATURATE = 448.0
PIECES = 4
LOGIT = 128 ** -0.5 * 1.4426950408889634
CUTS = ((0, 32), (32, 56), (56, 72))
QN = HEADS * ROWS
KV = HEADS * ROWS
SUMS = 16
LOGS = 8
SLACK = 64.0
STEPS = {1: ((256, 1024, 768, 256),), 2: ((256, 1024, 1024), (1024, 1024, 256))}
CAREFUL = 128
f32 = jnp.float32
bf16 = jnp.bfloat16


def pick_columns(first, count, parity):
    row = lax.broadcasted_iota(jnp.int32, (2 * HEADS, count * HD), 0)
    col = lax.broadcasted_iota(jnp.int32, (2 * HEADS, count * HD), 1)
    return (row == 2 * (first + col // HD) + parity).astype(f32).astype(bf16)


def rebuild(now, base, limit):
    base = base.astype(f32)
    residual = jnp.clip(now.astype(f32) - base, -limit, limit)
    return (base + residual.astype(bf16).astype(f32)).astype(bf16).astype(f32)


def pack_kernel(
    q_ref, kn_ref, vn_ref, kb_ref, vb_ref, code_ref, out_ref, held, held_codes, sems, code_sem
):
    width = HEADS // PIECES * HD
    code_copy = pltpu.make_async_copy(code_ref, held_codes, code_sem)
    code_copy.start()
    copies = []
    for p in range(PIECES):
        cols = slice(p * width, (p + 1) * width)
        copies.append([])
        for n, ref in enumerate((kn_ref, kb_ref, vn_ref, vb_ref, q_ref)):
            copy = pltpu.make_async_copy(ref.at[:, cols], held.at[n, :, cols], sems.at[p, n])
            copy.start()
            copies[p].append(copy)
    code_copy.wait()
    codes = held_codes[...]
    steps = jnp.left_shift(jnp.ones_like(codes), codes + 16).astype(f32)
    limits = (steps * (SATURATE / 65536.0)).astype(bf16)
    for p in range(PIECES):
        cols = slice(p * width, (p + 1) * width)
        made = []
        for parity in range(2):
            pick = pick_columns(p * HEADS // PIECES, HEADS // PIECES, parity)
            limit = lax.dot_general(
                limits, pick, (((0,), (0,)), ((), ())), preferred_element_type=f32
            )
            copies[p][2 * parity].wait()
            copies[p][2 * parity + 1].wait()
            made.append(rebuild(held[2 * parity, :, cols], held[2 * parity + 1, :, cols], limit))
        copies[p][4].wait()
        made.append(held[4, :, cols].astype(f32))
        for h in range(HEADS // PIECES):
            message = [part[:, h * HD : (h + 1) * HD] for part in made]
            out_ref[p * HEADS // PIECES + h] = jnp.concatenate(message, axis=0).astype(bf16)


def pack(*args):
    *arrays, codes = args
    arrays.append(codes.T)
    hbm = pl.BlockSpec(memory_space=pltpu.HBM)
    vmem = pl.BlockSpec(memory_space=pltpu.VMEM)
    return pl.pallas_call(
        pack_kernel,
        in_specs=[hbm] * 6,
        out_specs=vmem,
        out_shape=pltpu.VMEM((HEADS, 3 * ROWS, HD), bf16),
        scratch_shapes=[
            pltpu.VMEM((5, ROWS, HEADS * HD), bf16),
            pltpu.VMEM((2 * HEADS, ROWS), jnp.int32),
            pltpu.SemaphoreType.DMA((PIECES, 5)),
            pltpu.SemaphoreType.DMA,
        ],
        compiler_params=pltpu.CompilerParams(vmem_limit_bytes=16 * 2**20),
        name="pack",
    )(*(pltpu.with_memory_space_constraint(array, pltpu.HBM) for array in arrays))


def lay_out(rec_ref, k_ref, vt_ref):
    group = 16
    count = group * ROWS
    for g in range(HEADS // group):
        part = rec_ref[g * group : (g + 1) * group].astype(f32)
        keys = part[:, 0:ROWS].reshape(count, HD)
        values = part[:, ROWS : 2 * ROWS].reshape(count, HD)
        k_ref[g * count : (g + 1) * count, :] = keys.astype(bf16)
        vt_ref[0:HD, g * count : (g + 1) * count] = values.T.astype(bf16)
    vt_ref[HD : HD + SUMS, :] = jnp.ones((SUMS, KV), bf16)


def scale_queries(chunk):
    rows = chunk.reshape(HEADS * chunk.shape[1], HD) * LOGIT
    high = rows.astype(bf16)
    low = (rows - high.astype(f32)).astype(bf16)
    return jnp.concatenate([high, low], axis=1)


def attention(q, sets, held, store):
    def scores(k_ref, block):
        k = k_ref[block, :]
        k = jnp.concatenate([k, k], axis=1)
        return lax.dot_general(k, q, (((1,), (1,)), ((), ())), preferred_element_type=f32)

    def weigh(vt_ref, block, s, shift):
        weights = jnp.exp2(s - shift).astype(bf16)
        return jnp.dot(vt_ref[:, block], weights, preferred_element_type=f32)

    order = []
    for (k_ref, vt_ref), steps in zip(sets, STEPS[len(sets)]):
        for at, step in zip(itertools.accumulate(steps, initial=0), steps):
            order.append((k_ref, vt_ref, slice(at, at + step)))
    blocks = len(order)
    s = scores(order[0][0], order[0][2])
    shift = jnp.max(s, axis=0, keepdims=True) if held is None else held[0]
    total = None if held is None else held[1]
    largest = shift
    for n, (_, vt_ref, block) in enumerate(order):
        coming = scores(order[n + 1][0], order[n + 1][2]) if n + 1 < blocks else None
        if n or held is not None:
            largest = jnp.maximum(largest, jnp.max(s, axis=0, keepdims=True))
        part = weigh(vt_ref, block, s, shift)
        total = part if total is None else total + part
        s = coming
    store(shift, total)

    @pl.when(jnp.max(largest - shift) > SLACK)
    def _():
        if held is None:
            state = (jnp.full(shift.shape, -jnp.inf, f32), jnp.zeros(total.shape, f32))
        else:
            state = held
        for k_ref, vt_ref in sets:

            def step(j, state, k_ref=k_ref, vt_ref=vt_ref):
                top, total = state
                block = pl.ds(pl.multiple_of(j * CAREFUL, CAREFUL), CAREFUL)
                s = scores(k_ref, block)
                newer = jnp.maximum(top, jnp.max(s, axis=0, keepdims=True))
                return newer, total * jnp.exp2(top - newer) + weigh(vt_ref, block, s, newer)

            state = lax.fori_loop(0, KV // CAREFUL, step, state)
        store(*state)


def own_kernel(rec_ref, k_ref, vt_ref, *refs):
    lay_out(rec_ref, k_ref, vt_ref)
    count = len(CUTS)
    q_refs, shift_refs, total_refs = (refs[n * count : (n + 1) * count] for n in range(3))
    queries = rec_ref[...].astype(f32)[:, 2 * ROWS : 3 * ROWS]
    for n, (top, end) in enumerate(CUTS):
        q_refs[n][...] = scale_queries(queries[:, top:end])
    for n in range(count):

        def store(shift, total, n=n):
            shift_refs[n][...] = jnp.broadcast_to(shift, shift_refs[n].shape)
            total_refs[n][...] = total

        attention(q_refs[n][...], [(k_ref, vt_ref)], None, store)


def partner_kernel(lays_out, q_ref, k0_ref, vt0_ref, *refs):
    if lays_out:
        rec_ref, out_ref, k1_ref, vt1_ref = refs
        lay_out(rec_ref, k1_ref, vt1_ref)
    else:
        k1_ref, vt1_ref, out_ref = refs

    def store(shift, total):
        sums = total[HD : HD + 1]
        log = shift + jnp.log(sums) * 1.4426950408889634
        high = log.astype(bf16).astype(f32)
        middle = (log - high).astype(bf16).astype(f32)
        low = log - high - middle
        rest = jnp.zeros((LOGS - 3, log.shape[1]), f32)
        rows = [total[:HD] * (1.0 / sums), high, middle, low, rest]
        out_ref[...] = jnp.concatenate(rows, axis=0).astype(bf16)

    q = scale_queries(q_ref[...].astype(f32))
    attention(q, [(k0_ref, vt0_ref), (k1_ref, vt1_ref)], None, store)


def merge(shift, total, part_ref, out_ref):
    part = part_ref[...].astype(f32)
    log = part[HD : HD + 1] + part[HD + 1 : HD + 2] + part[HD + 2 : HD + 3]
    top = jnp.maximum(shift, log)
    mine, theirs = jnp.exp2(shift - top), jnp.exp2(log - top)
    sums = total[HD : HD + 1] * mine + theirs
    merged = total[:HD] * (mine / sums) + part[:HD] * (theirs / sums)
    out_ref[...] = merged.T.reshape(out_ref.shape).astype(bf16)


def last_kernel(q_ref, k_ref, vt_ref, shift_ref, total_ref, part_ref, out_ref):
    def store(shift, total):
        merge(shift, total, part_ref, out_ref)

    attention(q_ref[...], [(k_ref, vt_ref)], (shift_ref[0:1], total_ref[...]), store)


def other_kernel(q_ref, k_ref, vt_ref, shift_ref, total_ref, next_shift, next_total):
    def store(shift, total):
        next_shift[...] = jnp.broadcast_to(shift, next_shift.shape)
        next_total[...] = total

    attention(q_ref[...], [(k_ref, vt_ref)], (shift_ref[0:1], total_ref[...]), store)


def merge_kernel(shift_ref, total_ref, part_ref, out_ref):
    merge(shift_ref[0:1], total_ref[...], part_ref, out_ref)


VMEM = pl.BlockSpec(memory_space=pltpu.VMEM)
SIZES = [HEADS * (end - top) for top, end in CUTS]
QUERIES = [jax.ShapeDtypeStruct((n, 2 * HD), bf16) for n in SIZES]
KEYS = jax.ShapeDtypeStruct((KV, HD), bf16)
VALUES = jax.ShapeDtypeStruct((HD + SUMS, KV), bf16)
SHIFTS = [jax.ShapeDtypeStruct((8, n), f32) for n in SIZES]
TOTALS = [jax.ShapeDtypeStruct((HD + SUMS, n), f32) for n in SIZES]
PARTS = [jax.ShapeDtypeStruct((HD + LOGS, n), bf16) for n in SIZES]
OUTS = [jax.ShapeDtypeStruct((HEADS, end - top, HD), bf16) for top, end in CUTS]


def attend(kernel, name, outs, *args):
    return pl.pallas_call(
        kernel,
        in_specs=[VMEM] * len(args),
        out_specs=[VMEM] * len(outs),
        out_shape=outs,
        compiler_params=pltpu.CompilerParams(vmem_limit_bytes=24 * 2**20),
        cost_estimate=pl.CostEstimate(flops=0, bytes_accessed=0, transcendentals=0),
        name=name,
    )(*args)


def device(x, ylo, z, yhi, core):
    return (((x * 2 + ylo) * 4 + z) * 2 + yhi) * 2 + core


GROUPS = [
    [
        device(x, side ^ yhi, z, yhi, core)
        for x, z, yhi in itertools.product(range(4), range(4), range(2))
    ]
    for side, core in itertools.product(range(2), range(2))
]
PAIRS = {"chip": [], "core": []}
for x, ylo, z, yhi, core in itertools.product(range(4), range(2), range(4), range(2), range(2)):
    here = device(x, ylo, z, yhi, core)
    PAIRS["chip"].append((here, device(x, 1 - ylo, z, yhi, core)))
    PAIRS["core"].append((here, device(x, ylo, z, yhi, 1 - core)))


def exchange(messages):
    return lax.all_to_all(
        messages, "device", split_axis=0, concat_axis=0, axis_index_groups=GROUPS, tiled=True
    )


def swap(array, which):
    return lax.ppermute(array, "device", PAIRS[which])


def per_device(queries, keys_now, values_now, keys_base, values_base, scale_codes):
    own = exchange(pack(queries, keys_now, values_now, keys_base, values_base, scale_codes))
    theirs = [swap(own[:, 2 * ROWS + top : 2 * ROWS + end], "chip") for top, end in CUTS]
    theirs[1:] = lax.optimization_barrier(theirs[1:])
    other = swap(own, "core")
    count = len(CUTS)
    k0, vt0, *held = attend(own_kernel, "own", [KEYS, VALUES] + QUERIES + SHIFTS + TOTALS, own)
    held = [held[n::count] for n in range(count)]
    part, k1, vt1 = attend(
        functools.partial(partner_kernel, True),
        "partner_first", [PARTS[0], KEYS, VALUES], theirs[0], k0, vt0, other,
    )
    parts = [swap(part, "chip")]
    for n in range(1, count):
        (part,) = attend(
            functools.partial(partner_kernel, False),
            "partner", [PARTS[n]], theirs[n], k0, vt0, k1, vt1,
        )
        parts.append(swap(part, "chip"))
    merged = []
    for n in range(count):
        q, shift, total = held[n]
        if n + 1 < count:
            merged += attend(last_kernel, "last", [OUTS[n]], q, k1, vt1, shift, total, parts[n])
            merged[n], held[n + 1][0] = lax.optimization_barrier((merged[n], held[n + 1][0]))
        else:
            shift, total = attend(
                other_kernel, "other", [SHIFTS[n], TOTALS[n]], q, k1, vt1, shift, total
            )
            merged += attend(merge_kernel, "merge", [OUTS[n]], shift, total, parts[n])
    done = exchange(jnp.concatenate(merged, axis=1))
    return done.transpose(1, 0, 2).reshape(ROWS, HEADS * HD)


def solution(mesh):
    flat = Mesh(mesh.devices.reshape(-1), ("device",))
    rows = P("device", None)
    return jax.shard_map(
        per_device, mesh=flat, in_specs=(rows,) * 6, out_specs=rows, check_vma=False
    )
```

```python
import functools
import itertools

import jax
import jax.numpy as jnp
from jax import lax
from jax.experimental import pallas as pl
from jax.experimental.pallas import tpu as pltpu
from jax.sharding import Mesh
from jax.sharding import PartitionSpec as P

HEADS = 32
HD = 128
ROWS = 72
SATURATE = 448.0
PIECES = 4
LOGIT = 128 ** -0.5 * 1.4426950408889634
CUTS = ((0, 32), (32, 56), (56, 72))
QN = HEADS * ROWS
KV = HEADS * ROWS
SUMS = 16
LOGS = 8
SLACK = 64.0
STEPS = {1: ((256, 1024, 768, 256),), 2: ((256, 1024, 1024), (1024, 1024, 256))}
CAREFUL = 128
f32 = jnp.float32
bf16 = jnp.bfloat16


def pick_columns(count, parity):
    row = lax.broadcasted_iota(jnp.int32, (2 * count, count * HD), 0)
    col = lax.broadcasted_iota(jnp.int32, (2 * count, count * HD), 1)
    return (row == 2 * (col // HD) + parity).astype(f32).astype(bf16)


def rebuild(now, base, limit):
    base = base.astype(f32)
    residual = jnp.clip(now.astype(f32) - base, -limit, limit)
    return (base + residual.astype(bf16).astype(f32)).astype(bf16).astype(f32)


def pack_kernel(
    q_ref, kn_ref, vn_ref, kb_ref, vb_ref, code_ref, out_ref, held, held_codes, sems, code_sem
):
    width = HEADS // PIECES * HD
    code_copy = pltpu.make_async_copy(code_ref, held_codes, code_sem)
    code_copy.start()
    copies = []
    for p in range(PIECES):
        cols = slice(p * width, (p + 1) * width)
        copies.append([])
        for n, ref in enumerate((kn_ref, kb_ref, vn_ref, vb_ref, q_ref)):
            copy = pltpu.make_async_copy(ref.at[:, cols], held.at[n, :, cols], sems.at[p, n])
            copy.start()
            copies[p].append(copy)
    heads = HEADS // PIECES
    picks = [pick_columns(heads, parity) for parity in range(2)]
    code_copy.wait()
    codes = held_codes[...]
    steps = jnp.left_shift(jnp.ones_like(codes), codes + 16).astype(f32)
    limits = (steps * (SATURATE / 65536.0)).astype(bf16)
    for p in range(PIECES):
        cols = slice(p * width, (p + 1) * width)
        made = []
        for parity in range(2):
            limit = lax.dot_general(
                limits[2 * heads * p : 2 * heads * (p + 1)],
                picks[parity],
                (((0,), (0,)), ((), ())),
                preferred_element_type=f32,
            )
            copies[p][2 * parity].wait()
            copies[p][2 * parity + 1].wait()
            made.append(rebuild(held[2 * parity, :, cols], held[2 * parity + 1, :, cols], limit))
        copies[p][4].wait()
        made.append(held[4, :, cols].astype(f32))
        for h in range(heads):
            message = [part[:, h * HD : (h + 1) * HD] for part in made]
            out_ref[heads * p + h] = jnp.concatenate(message, axis=0).astype(bf16)


def pack(*args):
    *arrays, codes = args
    arrays.append(codes.T)
    hbm = pl.BlockSpec(memory_space=pltpu.HBM)
    vmem = pl.BlockSpec(memory_space=pltpu.VMEM)
    return pl.pallas_call(
        pack_kernel,
        in_specs=[hbm] * 6,
        out_specs=vmem,
        out_shape=pltpu.VMEM((HEADS, 3 * ROWS, HD), bf16),
        scratch_shapes=[
            pltpu.VMEM((5, ROWS, HEADS * HD), bf16),
            pltpu.VMEM((2 * HEADS, ROWS), jnp.int32),
            pltpu.SemaphoreType.DMA((PIECES, 5)),
            pltpu.SemaphoreType.DMA,
        ],
        compiler_params=pltpu.CompilerParams(vmem_limit_bytes=16 * 2**20),
        name="pack",
    )(*(pltpu.with_memory_space_constraint(array, pltpu.HBM) for array in arrays))


def lay_out(rec_ref, k_ref, vt_ref):
    group = 16
    count = group * ROWS
    for g in range(HEADS // group):
        part = rec_ref[g * group : (g + 1) * group].astype(f32)
        keys = part[:, 0:ROWS].reshape(count, HD)
        values = part[:, ROWS : 2 * ROWS].reshape(count, HD)
        k_ref[g * count : (g + 1) * count, :] = keys.astype(bf16)
        vt_ref[0:HD, g * count : (g + 1) * count] = values.T.astype(bf16)
    vt_ref[HD : HD + SUMS, :] = jnp.ones((SUMS, KV), bf16)


def scale_queries(chunk):
    rows = chunk.reshape(HEADS * chunk.shape[1], HD) * LOGIT
    high = rows.astype(bf16)
    low = (rows - high.astype(f32)).astype(bf16)
    return jnp.concatenate([high, low], axis=1)


def attention(q, sets, held, store):
    def scores(k_ref, block):
        k = k_ref[block, :]
        k = jnp.concatenate([k, k], axis=1)
        return lax.dot_general(k, q, (((1,), (1,)), ((), ())), preferred_element_type=f32)

    def weigh(vt_ref, block, s, shift):
        weights = jnp.exp2(s - shift).astype(bf16)
        return jnp.dot(vt_ref[:, block], weights, preferred_element_type=f32)

    order = []
    for (k_ref, vt_ref), steps in zip(sets, STEPS[len(sets)]):
        for at, step in zip(itertools.accumulate(steps, initial=0), steps):
            order.append((k_ref, vt_ref, slice(at, at + step)))
    blocks = len(order)
    s = scores(order[0][0], order[0][2])
    shift = jnp.max(s, axis=0, keepdims=True) if held is None else held[0]
    total = None if held is None else held[1]
    largest = shift
    for n, (_, vt_ref, block) in enumerate(order):
        coming = scores(order[n + 1][0], order[n + 1][2]) if n + 1 < blocks else None
        if n or held is not None:
            largest = jnp.maximum(largest, jnp.max(s, axis=0, keepdims=True))
        part = weigh(vt_ref, block, s, shift)
        total = part if total is None else total + part
        s = coming
    store(shift, total)

    @pl.when(jnp.max(largest - shift) > SLACK)
    def _():
        if held is None:
            state = (jnp.full(shift.shape, -jnp.inf, f32), jnp.zeros(total.shape, f32))
        else:
            state = held
        for k_ref, vt_ref in sets:

            def step(j, state, k_ref=k_ref, vt_ref=vt_ref):
                top, total = state
                block = pl.ds(pl.multiple_of(j * CAREFUL, CAREFUL), CAREFUL)
                s = scores(k_ref, block)
                newer = jnp.maximum(top, jnp.max(s, axis=0, keepdims=True))
                return newer, total * jnp.exp2(top - newer) + weigh(vt_ref, block, s, newer)

            state = lax.fori_loop(0, KV // CAREFUL, step, state)
        store(*state)


def own_kernel(rec_ref, k_ref, vt_ref, *refs):
    lay_out(rec_ref, k_ref, vt_ref)
    count = len(CUTS)
    q_refs, shift_refs, total_refs = (refs[n * count : (n + 1) * count] for n in range(3))
    queries = rec_ref[...].astype(f32)[:, 2 * ROWS : 3 * ROWS]
    for n, (top, end) in enumerate(CUTS):
        q_refs[n][...] = scale_queries(queries[:, top:end])
    for n in range(count):

        def store(shift, total, n=n):
            shift_refs[n][...] = jnp.broadcast_to(shift, shift_refs[n].shape)
            total_refs[n][...] = total

        attention(q_refs[n][...], [(k_ref, vt_ref)], None, store)


def partner_kernel(lays_out, q_ref, k0_ref, vt0_ref, *refs):
    if lays_out:
        rec_ref, out_ref, k1_ref, vt1_ref = refs
        lay_out(rec_ref, k1_ref, vt1_ref)
    else:
        k1_ref, vt1_ref, out_ref = refs

    def store(shift, total):
        sums = total[HD : HD + 1]
        log = shift + jnp.log(sums) * 1.4426950408889634
        high = log.astype(bf16).astype(f32)
        middle = (log - high).astype(bf16).astype(f32)
        low = log - high - middle
        rest = jnp.zeros((LOGS - 3, log.shape[1]), f32)
        rows = [total[:HD] * (1.0 / sums), high, middle, low, rest]
        out_ref[...] = jnp.concatenate(rows, axis=0).astype(bf16)

    q = scale_queries(q_ref[...].astype(f32))
    attention(q, [(k0_ref, vt0_ref), (k1_ref, vt1_ref)], None, store)


def merge(shift, total, part_ref, out_ref):
    part = part_ref[...].astype(f32)
    log = part[HD : HD + 1] + part[HD + 1 : HD + 2] + part[HD + 2 : HD + 3]
    top = jnp.maximum(shift, log)
    mine, theirs = jnp.exp2(shift - top), jnp.exp2(log - top)
    sums = total[HD : HD + 1] * mine + theirs
    merged = total[:HD] * (mine / sums) + part[:HD] * (theirs / sums)
    out_ref[...] = merged.T.reshape(out_ref.shape).astype(bf16)


def last_kernel(q_ref, k_ref, vt_ref, shift_ref, total_ref, part_ref, out_ref):
    def store(shift, total):
        merge(shift, total, part_ref, out_ref)

    attention(q_ref[...], [(k_ref, vt_ref)], (shift_ref[0:1], total_ref[...]), store)


def other_kernel(q_ref, k_ref, vt_ref, shift_ref, total_ref, next_shift, next_total):
    def store(shift, total):
        next_shift[...] = jnp.broadcast_to(shift, next_shift.shape)
        next_total[...] = total

    attention(q_ref[...], [(k_ref, vt_ref)], (shift_ref[0:1], total_ref[...]), store)


def merge_kernel(shift_ref, total_ref, part_ref, out_ref):
    merge(shift_ref[0:1], total_ref[...], part_ref, out_ref)


VMEM = pl.BlockSpec(memory_space=pltpu.VMEM)
SIZES = [HEADS * (end - top) for top, end in CUTS]
QUERIES = [jax.ShapeDtypeStruct((n, 2 * HD), bf16) for n in SIZES]
KEYS = jax.ShapeDtypeStruct((KV, HD), bf16)
VALUES = jax.ShapeDtypeStruct((HD + SUMS, KV), bf16)
SHIFTS = [jax.ShapeDtypeStruct((8, n), f32) for n in SIZES]
TOTALS = [jax.ShapeDtypeStruct((HD + SUMS, n), f32) for n in SIZES]
PARTS = [jax.ShapeDtypeStruct((HD + LOGS, n), bf16) for n in SIZES]
OUTS = [jax.ShapeDtypeStruct((HEADS, end - top, HD), bf16) for top, end in CUTS]


def attend(kernel, name, outs, *args):
    return pl.pallas_call(
        kernel,
        in_specs=[VMEM] * len(args),
        out_specs=[VMEM] * len(outs),
        out_shape=outs,
        compiler_params=pltpu.CompilerParams(vmem_limit_bytes=24 * 2**20),
        cost_estimate=pl.CostEstimate(flops=0, bytes_accessed=0, transcendentals=0),
        name=name,
    )(*args)


def device(x, ylo, z, yhi, core):
    return (((x * 2 + ylo) * 4 + z) * 2 + yhi) * 2 + core


GROUPS = [
    [
        device(x, side ^ yhi, z, yhi, core)
        for x, z, yhi in itertools.product(range(4), range(4), range(2))
    ]
    for side, core in itertools.product(range(2), range(2))
]
PAIRS = {"chip": [], "core": []}
for x, ylo, z, yhi, core in itertools.product(range(4), range(2), range(4), range(2), range(2)):
    here = device(x, ylo, z, yhi, core)
    PAIRS["chip"].append((here, device(x, 1 - ylo, z, yhi, core)))
    PAIRS["core"].append((here, device(x, ylo, z, yhi, 1 - core)))


def exchange(messages):
    return lax.all_to_all(
        messages, "device", split_axis=0, concat_axis=0, axis_index_groups=GROUPS, tiled=True
    )


def swap(array, which):
    return lax.ppermute(array, "device", PAIRS[which])


def per_device(queries, keys_now, values_now, keys_base, values_base, scale_codes):
    own = exchange(pack(queries, keys_now, values_now, keys_base, values_base, scale_codes))
    theirs = [swap(own[:, 2 * ROWS + top : 2 * ROWS + end], "chip") for top, end in CUTS]
    theirs[1:] = lax.optimization_barrier(theirs[1:])
    other = swap(own, "core")
    count = len(CUTS)
    k0, vt0, *held = attend(own_kernel, "own", [KEYS, VALUES] + QUERIES + SHIFTS + TOTALS, own)
    held = [held[n::count] for n in range(count)]
    part, k1, vt1 = attend(
        functools.partial(partner_kernel, True),
        "partner_first", [PARTS[0], KEYS, VALUES], theirs[0], k0, vt0, other,
    )
    parts = [swap(part, "chip")]
    for n in range(1, count):
        (part,) = attend(
            functools.partial(partner_kernel, False),
            "partner", [PARTS[n]], theirs[n], k0, vt0, k1, vt1,
        )
        parts.append(swap(part, "chip"))
    merged = []
    for n in range(count):
        q, shift, total = held[n]
        if n + 1 < count:
            merged += attend(last_kernel, "last", [OUTS[n]], q, k1, vt1, shift, total, parts[n])
            merged[n], held[n + 1][0] = lax.optimization_barrier((merged[n], held[n + 1][0]))
        else:
            shift, total = attend(
                other_kernel, "other", [SHIFTS[n], TOTALS[n]], q, k1, vt1, shift, total
            )
            merged += attend(merge_kernel, "merge", [OUTS[n]], shift, total, parts[n])
    done = exchange(jnp.concatenate(merged, axis=1))
    return done.transpose(1, 0, 2).reshape(ROWS, HEADS * HD)


def solution(mesh):
    flat = Mesh(mesh.devices.reshape(-1), ("device",))
    rows = P("device", None)
    return jax.shard_map(
        per_device, mesh=flat, in_specs=(rows,) * 6, out_specs=rows, check_vma=False
    )
```

```python
import functools
import itertools

import jax
import jax.numpy as jnp
from jax import lax
from jax.experimental import pallas as pl
from jax.experimental.pallas import tpu as pltpu
from jax.sharding import Mesh
from jax.sharding import PartitionSpec as P

HEADS = 32
HD = 128
ROWS = 72
SATURATE = 448.0
LOGIT = 128 ** -0.5 * 1.4426950408889634
CUTS = ((0, 32), (32, 56), (56, 72))
QN = HEADS * ROWS
KV = HEADS * ROWS
SUMS = 16
LOGS = 8
SLACK = 64.0
STEPS = {1: ((256, 1024, 768, 256),), 2: ((256, 1024, 1024), (1024, 1024, 256))}
CAREFUL = 128
f32 = jnp.float32
bf16 = jnp.bfloat16


def pick_columns(count, parity):
    row = lax.broadcasted_iota(jnp.int32, (2 * count, count * HD), 0)
    col = lax.broadcasted_iota(jnp.int32, (2 * count, count * HD), 1)
    return (row == 2 * (col // HD) + parity).astype(f32).astype(bf16)


def rebuild(now, base, limit):
    base = base.astype(f32)
    residual = jnp.clip(now.astype(f32) - base, -limit, limit)
    return (base + residual.astype(bf16).astype(f32)).astype(bf16).astype(f32)


def pack_kernel(heads, q_ref, kn_ref, vn_ref, kb_ref, vb_ref, code_ref, out_ref):
    codes = code_ref[...]
    steps = jnp.left_shift(jnp.ones_like(codes), codes + 16).astype(f32)
    limits = (steps * (SATURATE / 65536.0)).astype(bf16)
    made = []
    for parity, now_ref, base_ref in ((0, kn_ref, kb_ref), (1, vn_ref, vb_ref)):
        pick = pick_columns(heads, parity)
        limit = lax.dot_general(limits, pick, (((0,), (0,)), ((), ())), preferred_element_type=f32)
        made.append(rebuild(now_ref[...], base_ref[...], limit))
    made.append(q_ref[...].astype(f32))
    for h in range(heads):
        message = [part[:, h * HD : (h + 1) * HD] for part in made]
        out_ref[h] = jnp.concatenate(message, axis=0).astype(bf16)


def pack(queries, keys_now, values_now, keys_base, values_base, codes):
    heads = 16
    wide = pl.BlockSpec((ROWS, heads * HD), lambda i: (0, i))
    return pl.pallas_call(
        functools.partial(pack_kernel, heads),
        grid=(HEADS // heads,),
        in_specs=[wide] * 5 + [pl.BlockSpec((2 * heads, ROWS), lambda i: (i, 0))],
        out_specs=pl.BlockSpec((heads, 3 * ROWS, HD), lambda i: (i, 0, 0)),
        out_shape=jax.ShapeDtypeStruct((HEADS, 3 * ROWS, HD), bf16),
        compiler_params=pltpu.CompilerParams(vmem_limit_bytes=60 * 2**20),
        name="pack",
    )(queries, keys_now, values_now, keys_base, values_base, codes.T)


def lay_out(rec_ref, k_ref, vt_ref):
    group = 16
    count = group * ROWS
    for g in range(HEADS // group):
        part = rec_ref[g * group : (g + 1) * group].astype(f32)
        keys = part[:, 0:ROWS].reshape(count, HD)
        values = part[:, ROWS : 2 * ROWS].reshape(count, HD)
        k_ref[g * count : (g + 1) * count, :] = keys.astype(bf16)
        vt_ref[0:HD, g * count : (g + 1) * count] = values.T.astype(bf16)
    vt_ref[HD : HD + SUMS, :] = jnp.ones((SUMS, KV), bf16)


def scale_queries(chunk):
    rows = chunk.reshape(HEADS * chunk.shape[1], HD) * LOGIT
    high = rows.astype(bf16)
    low = (rows - high.astype(f32)).astype(bf16)
    return jnp.concatenate([high, low], axis=1)


def attention(q, sets, held, store):
    def scores(k_ref, block):
        k = k_ref[block, :]
        k = jnp.concatenate([k, k], axis=1)
        return lax.dot_general(k, q, (((1,), (1,)), ((), ())), preferred_element_type=f32)

    def weigh(vt_ref, block, s, shift):
        weights = jnp.exp2(s - shift).astype(bf16)
        return jnp.dot(vt_ref[:, block], weights, preferred_element_type=f32)

    order = []
    for (k_ref, vt_ref), steps in zip(sets, STEPS[len(sets)]):
        for at, step in zip(itertools.accumulate(steps, initial=0), steps):
            order.append((k_ref, vt_ref, slice(at, at + step)))
    blocks = len(order)
    s = scores(order[0][0], order[0][2])
    shift = jnp.max(s, axis=0, keepdims=True) if held is None else held[0]
    total = None if held is None else held[1]
    largest = shift
    for n, (_, vt_ref, block) in enumerate(order):
        coming = scores(order[n + 1][0], order[n + 1][2]) if n + 1 < blocks else None
        if n or held is not None:
            largest = jnp.maximum(largest, jnp.max(s, axis=0, keepdims=True))
        part = weigh(vt_ref, block, s, shift)
        total = part if total is None else total + part
        s = coming
    store(shift, total)

    @pl.when(jnp.max(largest - shift) > SLACK)
    def _():
        if held is None:
            state = (jnp.full(shift.shape, -jnp.inf, f32), jnp.zeros(total.shape, f32))
        else:
            state = held
        for k_ref, vt_ref in sets:

            def step(j, state, k_ref=k_ref, vt_ref=vt_ref):
                top, total = state
                block = pl.ds(pl.multiple_of(j * CAREFUL, CAREFUL), CAREFUL)
                s = scores(k_ref, block)
                newer = jnp.maximum(top, jnp.max(s, axis=0, keepdims=True))
                return newer, total * jnp.exp2(top - newer) + weigh(vt_ref, block, s, newer)

            state = lax.fori_loop(0, KV // CAREFUL, step, state)
        store(*state)


def own_kernel(rec_ref, k_ref, vt_ref, *refs):
    lay_out(rec_ref, k_ref, vt_ref)
    count = len(CUTS)
    q_refs, shift_refs, total_refs = (refs[n * count : (n + 1) * count] for n in range(3))
    queries = rec_ref[...].astype(f32)[:, 2 * ROWS : 3 * ROWS]
    for n, (top, end) in enumerate(CUTS):
        q_refs[n][...] = scale_queries(queries[:, top:end])
    for n in range(count):

        def store(shift, total, n=n):
            shift_refs[n][...] = jnp.broadcast_to(shift, shift_refs[n].shape)
            total_refs[n][...] = total

        attention(q_refs[n][...], [(k_ref, vt_ref)], None, store)


def partner_kernel(lays_out, q_ref, k0_ref, vt0_ref, *refs):
    if lays_out:
        rec_ref, out_ref, k1_ref, vt1_ref = refs
        lay_out(rec_ref, k1_ref, vt1_ref)
    else:
        k1_ref, vt1_ref, out_ref = refs

    def store(shift, total):
        sums = total[HD : HD + 1]
        log = shift + jnp.log(sums) * 1.4426950408889634
        high = log.astype(bf16).astype(f32)
        middle = (log - high).astype(bf16).astype(f32)
        low = log - high - middle
        rest = jnp.zeros((LOGS - 3, log.shape[1]), f32)
        rows = [total[:HD] * (1.0 / sums), high, middle, low, rest]
        out_ref[...] = jnp.concatenate(rows, axis=0).astype(bf16)

    q = scale_queries(q_ref[...].astype(f32))
    attention(q, [(k0_ref, vt0_ref), (k1_ref, vt1_ref)], None, store)


def merge(shift, total, part_ref, out_ref):
    part = part_ref[...].astype(f32)
    log = part[HD : HD + 1] + part[HD + 1 : HD + 2] + part[HD + 2 : HD + 3]
    top = jnp.maximum(shift, log)
    mine, theirs = jnp.exp2(shift - top), jnp.exp2(log - top)
    sums = total[HD : HD + 1] * mine + theirs
    merged = total[:HD] * (mine / sums) + part[:HD] * (theirs / sums)
    out_ref[...] = merged.T.reshape(out_ref.shape).astype(bf16)


def last_kernel(q_ref, k_ref, vt_ref, shift_ref, total_ref, part_ref, out_ref):
    def store(shift, total):
        merge(shift, total, part_ref, out_ref)

    attention(q_ref[...], [(k_ref, vt_ref)], (shift_ref[0:1], total_ref[...]), store)


def other_kernel(q_ref, k_ref, vt_ref, shift_ref, total_ref, next_shift, next_total):
    def store(shift, total):
        next_shift[...] = jnp.broadcast_to(shift, next_shift.shape)
        next_total[...] = total

    attention(q_ref[...], [(k_ref, vt_ref)], (shift_ref[0:1], total_ref[...]), store)


def merge_kernel(shift_ref, total_ref, part_ref, out_ref):
    merge(shift_ref[0:1], total_ref[...], part_ref, out_ref)


VMEM = pl.BlockSpec(memory_space=pltpu.VMEM)
SIZES = [HEADS * (end - top) for top, end in CUTS]
QUERIES = [jax.ShapeDtypeStruct((n, 2 * HD), bf16) for n in SIZES]
KEYS = jax.ShapeDtypeStruct((KV, HD), bf16)
VALUES = jax.ShapeDtypeStruct((HD + SUMS, KV), bf16)
SHIFTS = [jax.ShapeDtypeStruct((8, n), f32) for n in SIZES]
TOTALS = [jax.ShapeDtypeStruct((HD + SUMS, n), f32) for n in SIZES]
PARTS = [jax.ShapeDtypeStruct((HD + LOGS, n), bf16) for n in SIZES]
OUTS = [jax.ShapeDtypeStruct((HEADS, end - top, HD), bf16) for top, end in CUTS]


def attend(kernel, name, outs, *args):
    return pl.pallas_call(
        kernel,
        in_specs=[VMEM] * len(args),
        out_specs=[VMEM] * len(outs),
        out_shape=outs,
        compiler_params=pltpu.CompilerParams(vmem_limit_bytes=24 * 2**20),
        cost_estimate=pl.CostEstimate(flops=0, bytes_accessed=0, transcendentals=0),
        name=name,
    )(*args)


def device(x, ylo, z, yhi, core):
    return (((x * 2 + ylo) * 4 + z) * 2 + yhi) * 2 + core


GROUPS = [
    [
        device(x, side ^ yhi, z, yhi, core)
        for x, z, yhi in itertools.product(range(4), range(4), range(2))
    ]
    for side, core in itertools.product(range(2), range(2))
]
PAIRS = {"chip": [], "core": []}
for x, ylo, z, yhi, core in itertools.product(range(4), range(2), range(4), range(2), range(2)):
    here = device(x, ylo, z, yhi, core)
    PAIRS["chip"].append((here, device(x, 1 - ylo, z, yhi, core)))
    PAIRS["core"].append((here, device(x, ylo, z, yhi, 1 - core)))


def exchange(messages):
    return lax.all_to_all(
        messages, "device", split_axis=0, concat_axis=0, axis_index_groups=GROUPS, tiled=True
    )


def swap(array, which):
    return lax.ppermute(array, "device", PAIRS[which])


def per_device(queries, keys_now, values_now, keys_base, values_base, scale_codes):
    own = exchange(pack(queries, keys_now, values_now, keys_base, values_base, scale_codes))
    theirs = [swap(own[:, 2 * ROWS + top : 2 * ROWS + end], "chip") for top, end in CUTS]
    theirs[1:] = lax.optimization_barrier(theirs[1:])
    other = swap(own, "core")
    count = len(CUTS)
    k0, vt0, *held = attend(own_kernel, "own", [KEYS, VALUES] + QUERIES + SHIFTS + TOTALS, own)
    held = [held[n::count] for n in range(count)]
    part, k1, vt1 = attend(
        functools.partial(partner_kernel, True),
        "partner_first", [PARTS[0], KEYS, VALUES], theirs[0], k0, vt0, other,
    )
    parts = [swap(part, "chip")]
    for n in range(1, count):
        (part,) = attend(
            functools.partial(partner_kernel, False),
            "partner", [PARTS[n]], theirs[n], k0, vt0, k1, vt1,
        )
        parts.append(swap(part, "chip"))
    merged = []
    for n in range(count):
        q, shift, total = held[n]
        if n + 1 < count:
            merged += attend(last_kernel, "last", [OUTS[n]], q, k1, vt1, shift, total, parts[n])
            merged[n], held[n + 1][0] = lax.optimization_barrier((merged[n], held[n + 1][0]))
        else:
            shift, total = attend(
                other_kernel, "other", [SHIFTS[n], TOTALS[n]], q, k1, vt1, shift, total
            )
            merged += attend(merge_kernel, "merge", [OUTS[n]], shift, total, parts[n])
    done = exchange(jnp.concatenate(merged, axis=1))
    return done.transpose(1, 0, 2).reshape(ROWS, HEADS * HD)


def solution(mesh):
    flat = Mesh(mesh.devices.reshape(-1), ("device",))
    rows = P("device", None)
    return jax.shard_map(
        per_device, mesh=flat, in_specs=(rows,) * 6, out_specs=rows, check_vma=False
    )
```
